32 devices in a mesh: groups: 2 (over y), blk: 4 (over z), narrow: 4 (over x, core).
Axes of the slice: x: 2, y: 2, z: 4, core: 2. Of those that a mesh axis runs over, the one named last changes fastest.
Arguments:
- points: bfloat16 [8192, 128], P(('groups', 'blk', 'narrow')), parts along dimension 0, may hold values from -8 to 8
- inv_scale: float32 [128], replicated, may hold values from 0.08 to 0.25
- targets: float32 [8192, 64], P(('groups', 'blk', 'narrow')), parts along dimension 0, may hold values from -6 to 6
Outputs:
- solution: float32 [8192, 64], P(('groups', 'blk', 'narrow')), parts along dimension 0
- residual: float32 [8192, 64], P(('groups', 'blk', 'narrow')), parts along dimension 0
The draws below stay inside these ranges and needn't reach their ends.
There are 2 independent parts, one for each index of `groups`. The reference program is written for one: setup_inputs(seed, part) draws one part's arguments, and reference() takes and returns one part's arrays. A program takes and returns all parts, laid end to end along the dimension named above; an argument that names none is the same for every part. Nothing has to cross between parts.
All inputs are finite; a program needn't handle non-finite values.
Results may differ from the reference program's by a relative error of at most 0.0074.
Values may be sent and summed in bfloat16 or wider, within the bound.
No kernel may reach another device: no remote copies, remote signals or barrier semaphores. Data moves between devices by JAX's collectives and lax.ppermute only.
A program may use at most 64 MiB of HBM per device.

```python
import math
import jax
import jax.numpy as jnp
from jax import lax

FEATURES = 128
COLUMNS = 64
ITERATIONS = 2
POINTS = 4096


def draw_points(key, part):
    key = jax.random.fold_in(key, 11)
    subkeys = jax.random.split(key, 5)
    clusters = max(POINTS // 32, 2)
    member = jax.random.randint(subkeys[0], (POINTS,), 0, clusters)
    center_unit = jax.random.normal(subkeys[1], (clusters, FEATURES), jnp.float32)
    offset_unit = jax.random.normal(subkeys[2], (POINTS, FEATURES), jnp.float32)
    center_low = 0.6
    center_high = 2.2
    center_size = jnp.exp(jax.random.uniform(subkeys[3], (clusters, 1), jnp.float32, math.log(center_low), math.log(center_high)))
    offset_size = jnp.exp(jax.random.uniform(subkeys[4], (POINTS, 1), jnp.float32, math.log(0.1), math.log(0.5)))
    centers = center_size * center_unit
    placed = jnp.take(centers, member, axis=0) + offset_size * offset_unit
    return jnp.clip(placed, -8.0, 8.0).astype(jnp.bfloat16)


def level_of(stream_key, dims, shards, least, largest):
    gain = 1.0
    for position, blocks in shards:
        steps = jax.random.uniform(jax.random.fold_in(jax.random.fold_in(stream_key, 6), position), (blocks,), jnp.float32, least / len(shards), largest / len(shards))
        gain = gain * jnp.repeat(jnp.exp(steps), dims[position] // blocks).reshape((-1,) + (1,) * (len(dims) - 1 - position))
    return gain


def normal_values(key, shape, spread, reach, shards=(), kind=jnp.bfloat16):
    gain = level_of(key, shape, shards, -0.22, 0.18) if shards else 1.0
    array = jax.random.normal(key, shape, jnp.float32) * spread * gain
    return jnp.minimum(jnp.maximum(array, -reach), reach).astype(kind)


def setup_inputs(seed: int = 0, part: int = 0) -> dict:
    splits = jax.random.split(jax.random.key(seed), 4)
    own_keys = jax.random.split(jax.random.fold_in(splits[3], part), 4)
    points = draw_points(jax.random.fold_in(jax.random.fold_in(splits[3], part), 71), part)
    inv_scale = jnp.clip(jnp.exp(jax.random.uniform(splits[1], (FEATURES,), jnp.float32, math.log(0.08), math.log(0.25))), 0.08, 0.25)
    targets = normal_values(own_keys[2], (POINTS, COLUMNS), 1.0, 6.0, ((0, 16),), jnp.float32)
    return {"points": points, "inv_scale": inv_scale, "targets": targets}


noise_level = 1.0


def kernel_apply(scaled, sq, vector):
    row_count = math.gcd(scaled.shape[0], 1024)
    blocks = scaled.shape[0] // row_count
    row_blocks = scaled.reshape(blocks, row_count, scaled.shape[1])
    sq_blocks = sq.reshape(blocks, row_count)

    def one_block(pair):
        rows, row_sq = pair
        inner = lax.dot_general(rows, scaled, (((1,), (1,)), ((), ())), preferred_element_type=jnp.float32)
        tile = jnp.exp(-0.5 * (row_sq[:, None] + sq[None, :] - 2.0 * inner)).astype(jnp.bfloat16)
        return jnp.dot(tile, vector, preferred_element_type=jnp.float32)

    out = lax.map(one_block, (row_blocks, sq_blocks))
    return out.reshape(scaled.shape[0], vector.shape[1])


def reference(points, inv_scale, targets):
    scaled = (points.astype(jnp.float32) * inv_scale[None, :]).astype(jnp.bfloat16)
    sq = jnp.sum(jnp.square(scaled.astype(jnp.float32)), axis=1)
    solution = jnp.zeros_like(targets)
    residual = targets
    direction = targets
    norm_now = jnp.sum(residual * residual, axis=0)
    for step in range(ITERATIONS):
        image = kernel_apply(scaled, sq, direction.astype(jnp.bfloat16)) + noise_level * direction
        alpha = norm_now / jnp.sum(direction * image, axis=0)
        solution = solution + alpha[None, :] * direction
        residual = residual - alpha[None, :] * image
        norm_next = jnp.sum(residual * residual, axis=0)
        if step + 1 < ITERATIONS:
            direction = residual + (norm_next / norm_now)[None, :] * direction
            norm_now = norm_next
    return solution, residual
```

```python
import functools

import jax
import jax.numpy as jnp
from jax import lax
from jax.experimental import pallas as pl
from jax.experimental.pallas import tpu as pltpu
from jax.sharding import PartitionSpec as P

ITERATIONS = 2
noise_level = 1.0

BF16 = jnp.bfloat16
F32 = jnp.float32
LAST = (((1,), (1,)), ((), ()))
VMEM = pl.BlockSpec(memory_space=pltpu.VMEM)
LIMIT = 24 * 2**20


def call(kernel, outs, name, flops=0, exps=0, bytes_=0, scratch=()):
    return pl.pallas_call(
        kernel,
        out_shape=outs,
        out_specs=jax.tree.map(lambda _: VMEM, outs),
        scratch_shapes=list(scratch),
        name=name,
        cost_estimate=pl.CostEstimate(
            flops=flops, bytes_accessed=bytes_, transcendentals=exps
        ),
        compiler_params=pltpu.CompilerParams(vmem_limit_bytes=LIMIT),
    )


def pack_kernel(points_ref, scale_ref, targets_ref, pack_ref):
    n = points_ref.shape[0]
    half = n // 2
    m = targets_ref.shape[0]
    pack_ref[:n] = (points_ref[...].astype(F32) * scale_ref[...]).astype(BF16)
    pack_ref[n : n + m] = targets_ref[:, :half].astype(BF16)
    pack_ref[n + m :] = targets_ref[:, half:].astype(BF16)


def exponents(points, first):
    n, depth = points.shape
    value = -0.5 * jnp.sum(jnp.square(points.astype(F32)), axis=1, keepdims=True)
    high = value.astype(BF16).astype(F32)
    rest = value - high
    middle = rest.astype(BF16).astype(F32)
    low = rest - middle
    lane = lax.broadcasted_iota(jnp.int32, (n, depth), 1) - first
    other = lax.broadcasted_iota(jnp.int32, (n, depth), 1) - (3 - first)
    ones = jnp.where((other >= 0) & (other < 3), 1.0, 0.0)
    terms = jnp.where(lane == 0, high, jnp.where(lane == 1, middle, jnp.where(lane == 2, low, ones)))
    return terms.astype(BF16)


def fill(packs, n, first, out):
    depth = packs[0].shape[1]
    at = 0
    for ref in packs:
        for block in range(ref.shape[0] * 2 // (3 * n)):
            start = block * (n * 3 // 2)
            points = ref[start : start + n]
            out[at : at + n, :depth] = points
            out[at : at + n, depth:] = exponents(points, first)
            at += n


def vectors(packs, n, out):
    at = 0
    for ref in packs:
        for block in range(ref.shape[0] * 2 // (3 * n)):
            start = block * (n * 3 // 2) + n
            m = n // 4
            for part in range(2):
                out[:, at : at + n // 2] = ref[start + part * m : start + (part + 1) * m]
                at += n // 2


def make_tile(a_ref, b_ref, rows, cols, k_ref):
    step = min(rows, 512)

    def one(i, _):
        at = pl.multiple_of(i * step, step)
        inner = lax.dot_general(
            a_ref[pl.ds(at, step), :], b_ref[...], LAST, preferred_element_type=F32
        )
        k_ref[pl.ds(at, step), :] = jnp.exp(inner).astype(BF16)
        return 0

    lax.fori_loop(0, rows // step, one, 0)


def apply(vector_ref, k_ref, at, rows):
    return jnp.dot(
        vector_ref[:, at : at + rows], k_ref[...], preferred_element_type=F32
    )


def tile_kernel(n, n_rows, *refs):
    row_packs, (col_pack, *before, k_ref, y_ref, a, b, v) = refs[:n_rows], refs[n_rows:]
    fill(row_packs, n, 0, a)
    fill([col_pack], n, 3, b)
    vectors(row_packs, n, v)
    make_tile(a, b, a.shape[0], b.shape[0], k_ref)
    y = apply(v, k_ref, 0, a.shape[0])
    for ref in before:
        y = y + ref[...]
    y_ref[...] = y


def tile(n, m, row_packs, col_pack, before, name):
    depth = col_pack.shape[1]
    size = n + n // 2
    rows = sum(p.shape[0] for p in row_packs) // size * n
    cols = col_pack.shape[0] // size * n
    return call(
        functools.partial(tile_kernel, n, len(row_packs)),
        (jax.ShapeDtypeStruct((rows, cols), BF16), jax.ShapeDtypeStruct((m, cols), F32)),
        name,
        flops=rows * cols * (4 * depth + 2 * m),
        exps=rows * cols,
        bytes_=2 * rows * cols,
        scratch=[
            pltpu.VMEM((rows, 2 * depth), BF16),
            pltpu.VMEM((cols, 2 * depth), BF16),
            pltpu.VMEM((m, rows), BF16),
        ],
    )(*row_packs, col_pack, *before)


def columns_of(pieces, m):
    lane = lax.broadcasted_iota(jnp.int32, (m, 128), 1)
    out = jnp.zeros((m, 128), F32)
    for index, piece in enumerate(pieces):
        out = jnp.where(lane == index, piece, out)
    return out


def total(values):
    return jnp.sum(values, axis=1, keepdims=True)


def join_kernel(n, tz_ref, tx_ref, yz_ref, yx_ref, y_ref, sums_ref, v):
    vectors([tz_ref, tx_ref], n, v)
    half = yz_ref.shape[1]
    b = v[...].astype(F32)
    y_ref[:, :half] = yz_ref[...].astype(BF16)
    y_ref[:, half:] = yx_ref[...].astype(BF16)
    by = total(b[:, :half] * yz_ref[...]) + total(b[:, half:] * yx_ref[...])
    sums_ref[...] = columns_of([total(b * b), by], v.shape[0])


def first_step(mine, others):
    bb = mine[:, 0:1] + others[:, 0:1]
    by = mine[:, 1:2] + others[:, 1:2]
    bw = by + noise_level * bb
    return bb, bw, bb / bw


def second_kernel(
    n, tz_ref, tx_ref, yz_ref, yx_ref, y_ref, yu_ref, mine_ref, theirs_ref,
    kzz, kuz, kxz, kux, kx, kuxx, z_ref, sums_ref, v,
):
    half = yz_ref.shape[1]
    m = v.shape[0]
    vectors([tz_ref, tx_ref], n, v)
    _, _, a0 = first_step(mine_ref[...], theirs_ref[...])
    rows = kzz.shape[0]
    zz = (
        apply(y_ref, kzz, 0, rows) + apply(y_ref, kxz, rows, rows)
        + apply(yu_ref, kuz, 0, rows) + apply(yu_ref, kux, rows, rows)
    )
    yall = jnp.concatenate(
        [y_ref[:, :rows], yu_ref[:, :rows], y_ref[:, rows:]], axis=1
    )
    zx = jnp.dot(yall, kx[...], preferred_element_type=F32) + apply(
        yu_ref, kuxx, rows, rows
    )
    z_ref[...] = zz[:, :n]
    sums = [0.0] * 4
    for z, y, b in (
        (zz, yz_ref[...], v[:, :half].astype(F32)),
        (zx, yx_ref[...], v[:, half:].astype(F32)),
    ):
        w = y + noise_level * b
        r = b - a0 * w
        s = noise_level * r + (1.0 - noise_level * a0) * y - a0 * z
        for index, value in enumerate((r * r, r * s, b * s, r * w)):
            sums[index] = sums[index] + total(value)
    sums_ref[...] = columns_of(sums, m)


def last_kernel(
    n, b_ref, yz_ref, z_ref, mine_ref, theirs_ref, mine2_ref, theirs2_ref, x_ref, r_ref
):
    bb, bw, a0 = first_step(mine_ref[...], theirs_ref[...])
    sums = mine2_ref[...] + theirs2_ref[...]
    rr, rs, bs, rw = (sums[:, i : i + 1] for i in range(4))
    beta = rr / bb
    a1 = rr / (rs + beta * (bs + rw) + beta * beta * bw)
    b = b_ref[...]
    y = yz_ref[:, :n]
    r = b - a0 * (y + noise_level * b)
    p = r + beta * b
    image = (1.0 - noise_level * a0 + beta) * y - a0 * z_ref[...] + noise_level * p
    x_ref[...] = a0 * b + a1 * p
    r_ref[...] = r - a1 * image


def pair_body(blocks, points, inv_scale, targets):
    n, depth = points.shape
    m = targets.shape[1]
    own = targets.T

    def along(x, step):
        return lax.ppermute(x, "blk", [(i, i ^ step) for i in range(blocks)])

    def across(x):
        return lax.ppermute(x, "narrow", [(i, i ^ 2) for i in range(4)])

    def swap(x):
        return lax.ppermute(x, "narrow", [(i, i ^ 1) for i in range(4)])

    pack = call(
        pack_kernel, jax.ShapeDtypeStruct((n + 2 * m, depth), BF16), "pack"
    )(points, inv_scale[None, :], own)
    arrived = [pack] + [along(pack, step) for step in range(1, blocks)]
    tz = jnp.concatenate(arrived, axis=0)
    tx = jnp.concatenate([across(p) for p in arrived], axis=0)
    uz = swap(tz)
    ux = swap(tx)
    kzz, yz = tile(n, m, [tz], tz, [], "k_zz")
    kuz, yz = tile(n, m, [uz], tz, [yz], "k_uz")
    kx, yx = tile(n, m, [tz, uz, tx], tx, [], "k_x")
    kxz, yz = tile(n, m, [tx], tz, [yz], "k_xz")
    kux, yz = tile(n, m, [ux], tz, [yz], "k_ux_z")
    kuxx, yx = tile(n, m, [ux], tx, [yx], "k_ux_x")
    cols = yz.shape[1]
    vec = pltpu.VMEM((m, 2 * cols), BF16)
    sums_shape = jax.ShapeDtypeStruct((m, 128), F32)
    y, sums = call(
        functools.partial(join_kernel, n),
        (jax.ShapeDtypeStruct((m, 2 * cols), BF16), sums_shape),
        "join",
        scratch=[vec],
    )(tz, tx, yz, yx)
    yu = swap(y)
    sums_u = swap(sums)
    z, sums2 = call(
        functools.partial(second_kernel, n),
        (jax.ShapeDtypeStruct((m, n), F32), sums_shape),
        "second",
        scratch=[vec],
    )(tz, tx, yz, yx, y, yu, sums, sums_u, kzz, kuz, kxz, kux, kx, kuxx)
    sums2_u = swap(sums2)
    shape = jax.ShapeDtypeStruct((m, n), F32)
    x, r = call(functools.partial(last_kernel, n), (shape, shape), "last")(
        own, yz, z, sums, sums_u, sums2, sums2_u
    )
    return x.T, r.T


def spread_body(points, inv_scale, targets):
    def column_total(values):
        return lax.psum(jnp.sum(values, axis=0), ("blk", "narrow"))

    scaled = (points.astype(F32) * inv_scale[None, :]).astype(BF16)
    rows = lax.all_gather(scaled, "narrow", axis=0, tiled=True)
    columns = lax.all_gather(scaled, "blk", axis=0, tiled=True)
    row_sq = jnp.sum(jnp.square(rows.astype(F32)), axis=1)
    col_sq = jnp.sum(jnp.square(columns.astype(F32)), axis=1)
    inner = lax.dot_general(rows, columns, LAST, preferred_element_type=F32)
    kernel = jnp.exp(-0.5 * (row_sq[:, None] + col_sq[None, :] - 2.0 * inner)).astype(BF16)
    answer = jnp.zeros_like(targets)
    residual = targets
    direction = targets
    norm_now = column_total(residual * residual)
    for step in range(ITERATIONS):
        vector = lax.all_gather(direction.astype(BF16), "blk", axis=0, tiled=True)
        image = jnp.dot(kernel, vector, preferred_element_type=F32)
        image = lax.psum_scatter(image, "narrow", scatter_dimension=0, tiled=True)
        image = image + noise_level * direction
        alpha = norm_now / column_total(direction * image)
        answer = answer + alpha[None, :] * direction
        residual = residual - alpha[None, :] * image
        if step + 1 < ITERATIONS:
            norm_next = column_total(residual * residual)
            direction = residual + (norm_next / norm_now)[None, :] * direction
            norm_now = norm_next
    return answer, residual


def solution(mesh):
    blocks, narrow = mesh.shape["blk"], mesh.shape["narrow"]
    sharded = P(("groups", "blk", "narrow"), None)

    def whole(points, inv_scale, targets):
        fits = narrow == 4 and blocks in (1, 2, 4)
        n = points.shape[0] // mesh.size
        fits = fits and n * blocks <= 1024 and n == 4 * targets.shape[1]
        body = functools.partial(pair_body, blocks) if fits else spread_body
        return jax.shard_map(
            body,
            mesh=mesh,
            in_specs=(sharded, P(), sharded),
            out_specs=(sharded, sharded),
            check_vma=False,
        )(points, inv_scale, targets)

    return whole
```

```python
import functools

import jax
import jax.numpy as jnp
from jax import lax
from jax.experimental import pallas as pl
from jax.experimental.pallas import tpu as pltpu
from jax.sharding import PartitionSpec as P

ITERATIONS = 2
noise_level = 1.0

BF16 = jnp.bfloat16
F32 = jnp.float32
LAST = (((1,), (1,)), ((), ()))
VMEM = pl.BlockSpec(memory_space=pltpu.VMEM)
LIMIT = 20 * 2**20


def call(kernel, outs, name, flops=0, exps=0, bytes_=0, scratch=(), ins=None):
    return pl.pallas_call(
        kernel,
        **({} if ins is None else {"in_specs": ins}),
        out_shape=outs,
        out_specs=jax.tree.map(lambda _: VMEM, outs),
        scratch_shapes=list(scratch),
        name=name,
        cost_estimate=pl.CostEstimate(
            flops=flops, bytes_accessed=bytes_, transcendentals=exps
        ),
        compiler_params=pltpu.CompilerParams(vmem_limit_bytes=LIMIT),
    )


def pack_kernel(points_hbm, scale_hbm, targets_hbm, pack_ref, points_ref, scale_ref, targets_ref, sems):
    copies = [
        pltpu.make_async_copy(source, target, sems.at[index])
        for index, (source, target) in enumerate(
            ((points_hbm, points_ref), (scale_hbm, scale_ref), (targets_hbm, targets_ref))
        )
    ]
    for copy in copies:
        copy.start()
    for copy in copies:
        copy.wait()
    n = points_ref.shape[0]
    half = n // 2
    m = targets_ref.shape[0]
    pack_ref[:n] = (points_ref[...].astype(F32) * scale_ref[...]).astype(BF16)
    pack_ref[n : n + m] = targets_ref[:, :half].astype(BF16)
    pack_ref[n + m :] = targets_ref[:, half:].astype(BF16)


def exponents(points, first):
    n, depth = points.shape
    value = -0.5 * jnp.sum(jnp.square(points.astype(F32)), axis=1, keepdims=True)
    high = value.astype(BF16).astype(F32)
    rest = value - high
    middle = rest.astype(BF16).astype(F32)
    low = rest - middle
    lane = lax.broadcasted_iota(jnp.int32, (n, depth), 1) - first
    other = lax.broadcasted_iota(jnp.int32, (n, depth), 1) - (3 - first)
    ones = jnp.where((other >= 0) & (other < 3), 1.0, 0.0)
    terms = jnp.where(lane == 0, high, jnp.where(lane == 1, middle, jnp.where(lane == 2, low, ones)))
    return terms.astype(BF16)


def fill(packs, n, first, out):
    depth = packs[0].shape[1]
    at = 0
    for ref in packs:
        for block in range(ref.shape[0] * 2 // (3 * n)):
            start = block * (n * 3 // 2)
            points = ref[start : start + n]
            out[at : at + n, :depth] = points
            out[at : at + n, depth:] = exponents(points, first)
            at += n


def vectors(packs, n, out):
    at = 0
    for ref in packs:
        for block in range(ref.shape[0] * 2 // (3 * n)):
            start = block * (n * 3 // 2) + n
            m = n // 4
            for part in range(2):
                out[:, at : at + n // 2] = ref[start + part * m : start + (part + 1) * m]
                at += n // 2


def tile(a, b):
    return jnp.exp(lax.dot_general(a, b, LAST, preferred_element_type=F32)).astype(BF16)


def across_rows(v, k):
    return jnp.dot(v, k, preferred_element_type=F32)


def across_columns(v, k):
    return lax.dot_general(v, k, LAST, preferred_element_type=F32)


def early_kernel(n, z_ref, x_ref, a_ref, b_ref, v_ref, k_ref, y_ref):
    fill([z_ref, x_ref], n, 0, a_ref)
    fill([z_ref, x_ref], n, 3, b_ref)
    vectors([z_ref, x_ref], n, v_ref)
    k_ref[...] = tile(a_ref[...], b_ref[...])
    y_ref[...] = across_rows(v_ref[...], k_ref[...])


def early_other_kernel(n, u_ref, b_ref, y0_ref, a_ref, v_ref, k_ref, y_ref):
    fill([u_ref], n, 0, a_ref)
    vectors([u_ref], n, v_ref)
    k_ref[...] = tile(a_ref[...], b_ref[...])
    y_ref[...] = y0_ref[...] + across_rows(v_ref[...], k_ref[...])


def late_kernel(
    n, x_ref, ae_ref, au_ref, ve_ref, vu_ref, y0_ref, b_ref, v_ref, k_ref, ye_ref, yl_ref, a
):
    fill([x_ref], n, 0, a)
    fill([x_ref], n, 3, b_ref)
    vectors([x_ref], n, v_ref)
    early = ae_ref.shape[0]
    b = b_ref[...]
    k_ref[:early] = tile(ae_ref[...], b)
    k_ref[early : 2 * early] = tile(au_ref[...], b)
    k_ref[2 * early :] = tile(a[...], b)
    ye_ref[...] = y0_ref[...] + across_columns(v_ref[...], k_ref[:early])
    yl_ref[...] = (
        across_rows(ve_ref[...], k_ref[:early])
        + across_rows(vu_ref[...], k_ref[early : 2 * early])
        + across_rows(v_ref[...], k_ref[2 * early :])
    )


def columns_of(pieces, m):
    lane = lax.broadcasted_iota(jnp.int32, (m, 128), 1)
    out = jnp.zeros((m, 128), F32)
    for index, piece in enumerate(pieces):
        out = jnp.where(lane == index, piece, out)
    return out


def total(values):
    return jnp.sum(values, axis=1, keepdims=True)


def late_other_kernel(
    n, u_ref, be_ref, bl_ref, ve_ref, vl_ref, ye_ref, yl_ref,
    k_ref, y_ref, round_ref, sums_ref, a, v,
):
    fill([u_ref], n, 0, a)
    vectors([u_ref], n, v)
    early = be_ref.shape[0]
    k_ref[:, :early] = tile(a[...], be_ref[...])
    k_ref[:, early:] = tile(a[...], bl_ref[...])
    ye = ye_ref[...] + across_rows(v[...], k_ref[:, :early])
    yl = yl_ref[...] + across_rows(v[...], k_ref[:, early:])
    y_ref[:, :early] = ye
    y_ref[:, early:] = yl
    round_ref[:, :early] = ye.astype(BF16)
    round_ref[:, early:] = yl.astype(BF16)
    be = ve_ref[...].astype(F32)
    bl = vl_ref[...].astype(F32)
    sums_ref[...] = columns_of(
        [total(be * be) + total(bl * bl), total(be * ye) + total(bl * yl)], v.shape[0]
    )


def near_kernel(y_ref, ke_ref, kl_ref, z_ref):
    early = ke_ref.shape[0]
    ye, yl = y_ref[:, :early], y_ref[:, early:]
    z_ref[:, :early] = across_rows(ye, ke_ref[...]) + across_columns(yl, kl_ref[:early])
    z_ref[:, early:] = across_rows(ye, kl_ref[:early]) + across_rows(yl, kl_ref[2 * early :])


def first_step(mine, others):
    bb = mine[:, 0:1] + others[:, 0:1]
    by = mine[:, 1:2] + others[:, 1:2]
    bw = by + noise_level * bb
    return bb, bw, bb / bw


def far_kernel(
    n, y_ref, yu_ref, near_ref, mine_ref, theirs_ref, ve_ref, vl_ref, keu_ref, kl_ref, ku_ref,
    z_ref, sums_ref,
):
    early = keu_ref.shape[0]
    _, _, a0 = first_step(mine_ref[...], theirs_ref[...])
    ue, ul = yu_ref[:, :early], yu_ref[:, early:]
    ze = near_ref[:, :early] + across_rows(ue, keu_ref[...]) + across_rows(ul, ku_ref[:, :early])
    zl = (
        near_ref[:, early:]
        + across_rows(ue, kl_ref[early : 2 * early])
        + across_rows(ul, ku_ref[:, early:])
    )
    z_ref[...] = ze[:, :n]
    sums = [0.0] * 4
    for z, y, v in ((ze, y_ref[:, :early], ve_ref), (zl, y_ref[:, early:], vl_ref)):
        b = v[...].astype(F32)
        w = y + noise_level * b
        r = b - a0 * w
        s = noise_level * r + (1.0 - noise_level * a0) * y - a0 * z
        for index, value in enumerate((r * r, r * s, b * s, r * w)):
            sums[index] = sums[index] + total(value)
    sums_ref[...] = columns_of(sums, y_ref.shape[0])


def last_kernel(
    n, b_ref, y_ref, z_ref, mine_ref, theirs_ref, mine2_ref, theirs2_ref, x_ref, r_ref
):
    bb, bw, a0 = first_step(mine_ref[...], theirs_ref[...])
    sums = mine2_ref[...] + theirs2_ref[...]
    rr, rs, bs, rw = (sums[:, i : i + 1] for i in range(4))
    beta = rr / bb
    a1 = rr / (rs + beta * (bs + rw) + beta * beta * bw)
    b = b_ref[...]
    y = y_ref[:, :n]
    r = b - a0 * (y + noise_level * b)
    p = r + beta * b
    image = (1.0 - noise_level * a0 + beta) * y - a0 * z_ref[...] + noise_level * p
    x_ref[...] = a0 * b + a1 * p
    r_ref[...] = r - a1 * image


def pair_body(points, inv_scale, targets):
    n, depth = points.shape
    m = targets.shape[1]
    own = targets.T
    early, late = 6 * n, 2 * n

    def along(x, step):
        return lax.ppermute(x, "blk", [(i, i ^ step) for i in range(4)])

    def across(x):
        return lax.ppermute(x, "narrow", [(i, i ^ 2) for i in range(4)])

    def swap(x):
        return lax.ppermute(x, "narrow", [(i, i ^ 1) for i in range(4)])

    def f32(*shape):
        return jax.ShapeDtypeStruct(shape, F32)

    def bf16(*shape):
        return jax.ShapeDtypeStruct(shape, BF16)

    def named(kernel, outs, name, tiles=0, scratch=()):
        return call(
            functools.partial(kernel, n), outs, name,
            flops=tiles * (4 * depth + 2 * m), exps=tiles, bytes_=2 * tiles, scratch=scratch,
        )

    pack = call(
        pack_kernel, bf16(n + 2 * m, depth), "pack",
        scratch=[
            pltpu.VMEM((n, depth), BF16), pltpu.VMEM((1, depth), F32), pltpu.VMEM((m, n), F32),
            pltpu.SemaphoreType.DMA((3,)),
        ],
        ins=[pl.BlockSpec(memory_space=pltpu.HBM)] * 3,
    )(points, inv_scale[None, :], own)
    far = [along(pack, 3), along(pack, 2)]
    next_ = along(pack, 1)
    x_own = across(pack)
    x_next = across(next_)
    late_z = jnp.concatenate(far, axis=0)
    late_x = across(late_z)
    z_all = jnp.concatenate([pack, next_, late_z], axis=0)
    early_x = jnp.concatenate([x_own, x_next], axis=0)
    early_u = swap(jnp.concatenate([z_all, early_x], axis=0))
    a_e, b_e, v_e, k_e, y_e = named(
        early_kernel,
        (bf16(early, 2 * depth), bf16(early, 2 * depth), bf16(m, early), bf16(early, early), f32(m, early)),
        "early", early * early,
    )(z_all, early_x)
    a_u, v_u, k_eu, y_e = named(
        early_other_kernel,
        (bf16(early, 2 * depth), bf16(m, early), bf16(early, early), f32(m, early)),
        "early_other", early * early,
    )(early_u, b_e, y_e)
    late_x, y_e = lax.optimization_barrier((late_x, y_e))
    late_u = swap(late_x)
    b_l, v_l, k_l, y_e, y_l = named(
        late_kernel,
        (bf16(late, 2 * depth), bf16(m, late), bf16(2 * early + late, late), f32(m, early), f32(m, late)),
        "late", (2 * early + late) * late,
        scratch=[pltpu.VMEM((late, 2 * depth), BF16)],
    )(late_x, a_e, a_u, v_e, v_u, y_e)
    k_u, y, y_round, sums = named(
        late_other_kernel,
        (bf16(late, early + late), f32(m, early + late), bf16(m, early + late), f32(m, 128)),
        "late_other", late * (early + late),
        scratch=[pltpu.VMEM((late, 2 * depth), BF16), pltpu.VMEM((m, late), BF16)],
    )(late_u, b_e, b_l, v_e, v_l, y_e, y_l)
    y_u = swap(y_round)
    sums_u = swap(sums)
    near = call(
        near_kernel, f32(m, early + late), "near", flops=2 * m * (early + late) ** 2
    )(y_round, k_e, k_l)
    z, sums2 = named(far_kernel, (f32(m, n), f32(m, 128)), "far")(
        y, y_u, near, sums, sums_u, v_e, v_l, k_eu, k_l, k_u
    )
    sums2_u = swap(sums2)
    x, r = named(last_kernel, (f32(m, n), f32(m, n)), "last")(
        own, y, z, sums, sums_u, sums2, sums2_u
    )
    return x.T, r.T


def spread_body(points, inv_scale, targets):
    def column_total(values):
        return lax.psum(jnp.sum(values, axis=0), ("blk", "narrow"))

    scaled = (points.astype(F32) * inv_scale[None, :]).astype(BF16)
    rows = lax.all_gather(scaled, "narrow", axis=0, tiled=True)
    columns = lax.all_gather(scaled, "blk", axis=0, tiled=True)
    row_sq = jnp.sum(jnp.square(rows.astype(F32)), axis=1)
    col_sq = jnp.sum(jnp.square(columns.astype(F32)), axis=1)
    inner = lax.dot_general(rows, columns, LAST, preferred_element_type=F32)
    kernel = jnp.exp(-0.5 * (row_sq[:, None] + col_sq[None, :] - 2.0 * inner)).astype(BF16)
    answer = jnp.zeros_like(targets)
    residual = targets
    direction = targets
    norm_now = column_total(residual * residual)
    for step in range(ITERATIONS):
        vector = lax.all_gather(direction.astype(BF16), "blk", axis=0, tiled=True)
        image = jnp.dot(kernel, vector, preferred_element_type=F32)
        image = lax.psum_scatter(image, "narrow", scatter_dimension=0, tiled=True)
        image = image + noise_level * direction
        alpha = norm_now / column_total(direction * image)
        answer = answer + alpha[None, :] * direction
        residual = residual - alpha[None, :] * image
        if step + 1 < ITERATIONS:
            norm_next = column_total(residual * residual)
            direction = residual + (norm_next / norm_now)[None, :] * direction
            norm_now = norm_next
    return answer, residual


def solution(mesh):
    blocks, narrow = mesh.shape["blk"], mesh.shape["narrow"]
    sharded = P(("groups", "blk", "narrow"), None)

    def whole(points, inv_scale, targets):
        n = points.shape[0] // mesh.size
        fits = narrow == 4 and blocks == 4 and n <= 256 and n == 4 * targets.shape[1]
        body = pair_body if fits else spread_body
        return jax.shard_map(
            body,
            mesh=mesh,
            in_specs=(sharded, P(), sharded),
            out_specs=(sharded, sharded),
            check_vma=False,
        )(points, inv_scale, targets)

    return whole
```

```python
import functools

import jax
import jax.numpy as jnp
from jax import lax
from jax.experimental import pallas as pl
from jax.experimental.pallas import tpu as pltpu
from jax.sharding import PartitionSpec as P

ITERATIONS = 2
noise_level = 1.0

BF16 = jnp.bfloat16
F32 = jnp.float32
LAST = (((1,), (1,)), ((), ()))
VMEM = pl.BlockSpec(memory_space=pltpu.VMEM)
LIMIT = 20 * 2**20


def call(kernel, outs, name, flops=0, exps=0, bytes_=0, scratch=()):
    return pl.pallas_call(
        kernel,
        out_shape=outs,
        out_specs=jax.tree.map(lambda _: VMEM, outs),
        scratch_shapes=list(scratch),
        name=name,
        cost_estimate=pl.CostEstimate(
            flops=flops, bytes_accessed=bytes_, transcendentals=exps
        ),
        compiler_params=pltpu.CompilerParams(vmem_limit_bytes=LIMIT),
    )


def exponents(points, first):
    n, depth = points.shape
    value = -0.5 * jnp.sum(jnp.square(points.astype(F32)), axis=1, keepdims=True)
    high = value.astype(BF16).astype(F32)
    rest = value - high
    middle = rest.astype(BF16).astype(F32)
    low = rest - middle
    lane = lax.broadcasted_iota(jnp.int32, (n, depth), 1) - first
    other = lax.broadcasted_iota(jnp.int32, (n, depth), 1) - (3 - first)
    ones = jnp.where((other >= 0) & (other < 3), 1.0, 0.0)
    terms = jnp.where(lane == 0, high, jnp.where(lane == 1, middle, jnp.where(lane == 2, low, ones)))
    return terms.astype(BF16)


def fill(packs, n, first, out):
    depth = packs[0].shape[1]
    at = 0
    for ref in packs:
        for block in range(ref.shape[0] * 2 // (3 * n)):
            start = block * (n * 3 // 2)
            points = ref[start : start + n]
            out[at : at + n, :depth] = points
            out[at : at + n, depth:] = exponents(points, first)
            at += n


def vectors(packs, n, out):
    at = 0
    for ref in packs:
        for block in range(ref.shape[0] * 2 // (3 * n)):
            start = block * (n * 3 // 2) + n
            m = n // 4
            for part in range(2):
                out[:, at : at + n // 2] = ref[start + part * m : start + (part + 1) * m]
                at += n // 2


def tile(a, b):
    return jnp.exp(lax.dot_general(a, b, LAST, preferred_element_type=F32)).astype(BF16)


def across_rows(v, k):
    return jnp.dot(v, k, preferred_element_type=F32)


def across_columns(v, k):
    return lax.dot_general(v, k, LAST, preferred_element_type=F32)


def early_kernel(n, z_ref, x_ref, a_ref, b_ref, v_ref, k_ref, y_ref):
    fill([z_ref, x_ref], n, 0, a_ref)
    fill([z_ref, x_ref], n, 3, b_ref)
    vectors([z_ref, x_ref], n, v_ref)
    k_ref[...] = tile(a_ref[...], b_ref[...])
    y_ref[...] = across_rows(v_ref[...], k_ref[...])


def early_other_kernel(n, u_ref, b_ref, y0_ref, a_ref, v_ref, k_ref, y_ref):
    fill([u_ref], n, 0, a_ref)
    vectors([u_ref], n, v_ref)
    k_ref[...] = tile(a_ref[...], b_ref[...])
    y_ref[...] = y0_ref[...] + across_rows(v_ref[...], k_ref[...])


def late_kernel(
    n, x_ref, ae_ref, au_ref, ve_ref, vu_ref, y0_ref, b_ref, v_ref, k_ref, ye_ref, yl_ref, a
):
    fill([x_ref], n, 0, a)
    fill([x_ref], n, 3, b_ref)
    vectors([x_ref], n, v_ref)
    early = ae_ref.shape[0]
    b = b_ref[...]
    k_ref[:early] = tile(ae_ref[...], b)
    k_ref[early : 2 * early] = tile(au_ref[...], b)
    k_ref[2 * early :] = tile(a[...], b)
    ye_ref[...] = y0_ref[...] + across_columns(v_ref[...], k_ref[:early])
    yl_ref[...] = (
        across_rows(ve_ref[...], k_ref[:early])
        + across_rows(vu_ref[...], k_ref[early : 2 * early])
        + across_rows(v_ref[...], k_ref[2 * early :])
    )


def columns_of(pieces, m):
    lane = lax.broadcasted_iota(jnp.int32, (m, 128), 1)
    out = jnp.zeros((m, 128), F32)
    for index, piece in enumerate(pieces):
        out = jnp.where(lane == index, piece, out)
    return out


def total(values):
    return jnp.sum(values, axis=1, keepdims=True)


def late_other_kernel(
    n, u_ref, be_ref, bl_ref, ve_ref, vl_ref, ye_ref, yl_ref,
    k_ref, y_ref, round_ref, sums_ref, a, v,
):
    fill([u_ref], n, 0, a)
    vectors([u_ref], n, v)
    early = be_ref.shape[0]
    k_ref[:, :early] = tile(a[...], be_ref[...])
    k_ref[:, early:] = tile(a[...], bl_ref[...])
    ye = ye_ref[...] + across_rows(v[...], k_ref[:, :early])
    yl = yl_ref[...] + across_rows(v[...], k_ref[:, early:])
    y_ref[:, :early] = ye
    y_ref[:, early:] = yl
    round_ref[:, :early] = ye.astype(BF16)
    round_ref[:, early:] = yl.astype(BF16)
    be = ve_ref[...].astype(F32)
    bl = vl_ref[...].astype(F32)
    sums_ref[...] = columns_of(
        [total(be * be) + total(bl * bl), total(be * ye) + total(bl * yl)], v.shape[0]
    )


def near_kernel(y_ref, ke_ref, kl_ref, z_ref):
    early = ke_ref.shape[0]
    ye, yl = y_ref[:, :early], y_ref[:, early:]
    z_ref[:, :early] = across_rows(ye, ke_ref[...]) + across_columns(yl, kl_ref[:early])
    z_ref[:, early:] = across_rows(ye, kl_ref[:early]) + across_rows(yl, kl_ref[2 * early :])


def first_step(mine, others):
    bb = mine[:, 0:1] + others[:, 0:1]
    by = mine[:, 1:2] + others[:, 1:2]
    bw = by + noise_level * bb
    return bb, bw, bb / bw


def far_kernel(
    n, y_ref, yu_ref, near_ref, mine_ref, theirs_ref, ve_ref, vl_ref, keu_ref, kl_ref, ku_ref,
    z_ref, sums_ref,
):
    early = keu_ref.shape[0]
    _, _, a0 = first_step(mine_ref[...], theirs_ref[...])
    ue, ul = yu_ref[:, :early], yu_ref[:, early:]
    ze = near_ref[:, :early] + across_rows(ue, keu_ref[...]) + across_rows(ul, ku_ref[:, :early])
    zl = (
        near_ref[:, early:]
        + across_rows(ue, kl_ref[early : 2 * early])
        + across_rows(ul, ku_ref[:, early:])
    )
    z_ref[...] = ze[:, :n]
    sums = [0.0] * 4
    for z, y, v in ((ze, y_ref[:, :early], ve_ref), (zl, y_ref[:, early:], vl_ref)):
        b = v[...].astype(F32)
        w = y + noise_level * b
        r = b - a0 * w
        s = noise_level * r + (1.0 - noise_level * a0) * y - a0 * z
        for index, value in enumerate((r * r, r * s, b * s, r * w)):
            sums[index] = sums[index] + total(value)
    sums_ref[...] = columns_of(sums, y_ref.shape[0])


def last_kernel(
    n, b_ref, y_ref, z_ref, mine_ref, theirs_ref, mine2_ref, theirs2_ref, x_ref, r_ref
):
    bb, bw, a0 = first_step(mine_ref[...], theirs_ref[...])
    sums = mine2_ref[...] + theirs2_ref[...]
    rr, rs, bs, rw = (sums[:, i : i + 1] for i in range(4))
    beta = rr / bb
    a1 = rr / (rs + beta * (bs + rw) + beta * beta * bw)
    b = b_ref[...]
    y = y_ref[:, :n]
    r = b - a0 * (y + noise_level * b)
    p = r + beta * b
    image = (1.0 - noise_level * a0 + beta) * y - a0 * z_ref[...] + noise_level * p
    x_ref[...] = a0 * b + a1 * p
    r_ref[...] = r - a1 * image


def pair_body(points, inv_scale, targets):
    n, depth = points.shape
    m = targets.shape[1]
    own = targets.T
    early, late = 6 * n, 2 * n

    def along(x, step):
        return lax.ppermute(x, "blk", [(i, i ^ step) for i in range(4)])

    def across(x):
        return lax.ppermute(x, "narrow", [(i, i ^ 2) for i in range(4)])

    def swap(x):
        return lax.ppermute(x, "narrow", [(i, i ^ 1) for i in range(4)])

    def f32(*shape):
        return jax.ShapeDtypeStruct(shape, F32)

    def bf16(*shape):
        return jax.ShapeDtypeStruct(shape, BF16)

    def named(kernel, outs, name, tiles=0, scratch=()):
        return call(
            functools.partial(kernel, n), outs, name,
            flops=tiles * (4 * depth + 2 * m), exps=tiles, bytes_=2 * tiles, scratch=scratch,
        )

    scaled = (points.astype(F32) * inv_scale[None, :]).astype(BF16)
    rounded = own.astype(BF16)
    pack = jnp.concatenate([scaled, rounded[:, : n // 2], rounded[:, n // 2 :]], axis=0)
    far = [along(pack, 3), along(pack, 2)]
    next_ = along(pack, 1)
    x_own = across(pack)
    x_next = across(next_)
    late_z = jnp.concatenate(far, axis=0)
    late_x = across(late_z)
    z_all = jnp.concatenate([pack, next_, late_z], axis=0)
    early_x = jnp.concatenate([x_own, x_next], axis=0)
    early_u = swap(jnp.concatenate([z_all, early_x], axis=0))
    a_e, b_e, v_e, k_e, y_e = named(
        early_kernel,
        (bf16(early, 2 * depth), bf16(early, 2 * depth), bf16(m, early), bf16(early, early), f32(m, early)),
        "early", early * early,
    )(z_all, early_x)
    a_u, v_u, k_eu, y_e = named(
        early_other_kernel,
        (bf16(early, 2 * depth), bf16(m, early), bf16(early, early), f32(m, early)),
        "early_other", early * early,
    )(early_u, b_e, y_e)
    late_x, y_e = lax.optimization_barrier((late_x, y_e))
    late_u = swap(late_x)
    b_l, v_l, k_l, y_e, y_l = named(
        late_kernel,
        (bf16(late, 2 * depth), bf16(m, late), bf16(2 * early + late, late), f32(m, early), f32(m, late)),
        "late", (2 * early + late) * late,
        scratch=[pltpu.VMEM((late, 2 * depth), BF16)],
    )(late_x, a_e, a_u, v_e, v_u, y_e)
    k_u, y, y_round, sums = named(
        late_other_kernel,
        (bf16(late, early + late), f32(m, early + late), bf16(m, early + late), f32(m, 128)),
        "late_other", late * (early + late),
        scratch=[pltpu.VMEM((late, 2 * depth), BF16), pltpu.VMEM((m, late), BF16)],
    )(late_u, b_e, b_l, v_e, v_l, y_e, y_l)
    y_u = swap(y_round)
    sums_u = swap(sums)
    near = call(
        near_kernel, f32(m, early + late), "near", flops=2 * m * (early + late) ** 2
    )(y_round, k_e, k_l)
    z, sums2 = named(far_kernel, (f32(m, n), f32(m, 128)), "far")(
        y, y_u, near, sums, sums_u, v_e, v_l, k_eu, k_l, k_u
    )
    sums2_u = swap(sums2)
    x, r = named(last_kernel, (f32(m, n), f32(m, n)), "last")(
        own, y, z, sums, sums_u, sums2, sums2_u
    )
    return x.T, r.T


def spread_body(points, inv_scale, targets):
    def column_total(values):
        return lax.psum(jnp.sum(values, axis=0), ("blk", "narrow"))

    scaled = (points.astype(F32) * inv_scale[None, :]).astype(BF16)
    rows = lax.all_gather(scaled, "narrow", axis=0, tiled=True)
    columns = lax.all_gather(scaled, "blk", axis=0, tiled=True)
    row_sq = jnp.sum(jnp.square(rows.astype(F32)), axis=1)
    col_sq = jnp.sum(jnp.square(columns.astype(F32)), axis=1)
    inner = lax.dot_general(rows, columns, LAST, preferred_element_type=F32)
    kernel = jnp.exp(-0.5 * (row_sq[:, None] + col_sq[None, :] - 2.0 * inner)).astype(BF16)
    answer = jnp.zeros_like(targets)
    residual = targets
    direction = targets
    norm_now = column_total(residual * residual)
    for step in range(ITERATIONS):
        vector = lax.all_gather(direction.astype(BF16), "blk", axis=0, tiled=True)
        image = jnp.dot(kernel, vector, preferred_element_type=F32)
        image = lax.psum_scatter(image, "narrow", scatter_dimension=0, tiled=True)
        image = image + noise_level * direction
        alpha = norm_now / column_total(direction * image)
        answer = answer + alpha[None, :] * direction
        residual = residual - alpha[None, :] * image
        if step + 1 < ITERATIONS:
            norm_next = column_total(residual * residual)
            direction = residual + (norm_next / norm_now)[None, :] * direction
            norm_now = norm_next
    return answer, residual


def solution(mesh):
    blocks, narrow = mesh.shape["blk"], mesh.shape["narrow"]
    sharded = P(("groups", "blk", "narrow"), None)

    def whole(points, inv_scale, targets):
        n = points.shape[0] // mesh.size
        fits = narrow == 4 and blocks == 4 and n <= 256 and n == 4 * targets.shape[1]
        body = pair_body if fits else spread_body
        return jax.shard_map(
            body,
            mesh=mesh,
            in_specs=(sharded, P(), sharded),
            out_specs=(sharded, sharded),
            check_vma=False,
        )(points, inv_scale, targets)

    return whole
```

```python
import functools

import jax
import jax.numpy as jnp
from jax import lax
from jax.experimental import pallas as pl
from jax.experimental.pallas import tpu as pltpu
from jax.sharding import PartitionSpec as P

ITERATIONS = 2
noise_level = 1.0

BF16 = jnp.bfloat16
F32 = jnp.float32
LAST = (((1,), (1,)), ((), ()))
VMEM = pl.BlockSpec(memory_space=pltpu.VMEM)
LIMIT = 20 * 2**20


def call(kernel, outs, name, flops=0, exps=0, bytes_=0, scratch=()):
    return pl.pallas_call(
        kernel,
        out_shape=outs,
        out_specs=jax.tree.map(lambda _: VMEM, outs),
        scratch_shapes=list(scratch),
        name=name,
        cost_estimate=pl.CostEstimate(
            flops=flops, bytes_accessed=bytes_, transcendentals=exps
        ),
        compiler_params=pltpu.CompilerParams(vmem_limit_bytes=LIMIT),
    )


def exponents(points, first):
    n, depth = points.shape
    value = -0.5 * jnp.sum(jnp.square(points.astype(F32)), axis=1, keepdims=True)
    high = value.astype(BF16).astype(F32)
    rest = value - high
    middle = rest.astype(BF16).astype(F32)
    low = rest - middle
    lane = lax.broadcasted_iota(jnp.int32, (n, depth), 1) - first
    other = lax.broadcasted_iota(jnp.int32, (n, depth), 1) - (3 - first)
    ones = jnp.where((other >= 0) & (other < 3), 1.0, 0.0)
    terms = jnp.where(lane == 0, high, jnp.where(lane == 1, middle, jnp.where(lane == 2, low, ones)))
    return terms.astype(BF16)


def fill(packs, n, first, out):
    depth = packs[0].shape[1]
    at = 0
    for ref in packs:
        for block in range(ref.shape[0] // (2 * n)):
            start = block * 2 * n
            points = ref[start : start + n]
            out[at : at + n, :depth] = points
            out[at : at + n, depth:] = exponents(points, first)
            at += n


def vectors(packs, n, out, low=False):
    at = 0
    m = n // 4
    for ref in packs:
        for block in range(ref.shape[0] // (2 * n)):
            start = block * 2 * n + n
            for part in range(2):
                value = ref[start + part * m : start + (part + 1) * m]
                if low:
                    rest = ref[start + (part + 2) * m : start + (part + 3) * m]
                    value = value.astype(F32) + rest.astype(F32)
                out[:, at : at + n // 2] = value
                at += n // 2


def tile(a, b):
    return jnp.exp(lax.dot_general(a, b, LAST, preferred_element_type=F32)).astype(BF16)


def across_rows(v, k):
    return jnp.dot(v, k, preferred_element_type=F32)


def across_columns(v, k):
    return lax.dot_general(v, k, LAST, preferred_element_type=F32)


def early_kernel(n, z_ref, x_ref, a_ref, b_ref, v_ref, k_ref, y_ref):
    fill([z_ref, x_ref], n, 0, a_ref)
    fill([z_ref, x_ref], n, 3, b_ref)
    vectors([z_ref, x_ref], n, v_ref)
    k_ref[...] = tile(a_ref[...], b_ref[...])
    y_ref[...] = across_rows(v_ref[...], k_ref[...])


def early_other_kernel(n, u_ref, b_ref, y0_ref, a_ref, v_ref, k_ref, y_ref):
    fill([u_ref], n, 0, a_ref)
    vectors([u_ref], n, v_ref)
    k_ref[...] = tile(a_ref[...], b_ref[...])
    y_ref[...] = y0_ref[...] + across_rows(v_ref[...], k_ref[...])


def late_kernel(
    n, x_ref, ae_ref, au_ref, ve_ref, vu_ref, y0_ref, b_ref, v_ref, k_ref, ye_ref, yl_ref, a
):
    fill([x_ref], n, 0, a)
    fill([x_ref], n, 3, b_ref)
    vectors([x_ref], n, v_ref)
    early = ae_ref.shape[0]
    b = b_ref[...]
    k_ref[:early] = tile(ae_ref[...], b)
    k_ref[early : 2 * early] = tile(au_ref[...], b)
    k_ref[2 * early :] = tile(a[...], b)
    ye_ref[...] = y0_ref[...] + across_columns(v_ref[...], k_ref[:early])
    yl_ref[...] = (
        across_rows(ve_ref[...], k_ref[:early])
        + across_rows(vu_ref[...], k_ref[early : 2 * early])
        + across_rows(v_ref[...], k_ref[2 * early :])
    )


def columns_of(pieces, m):
    lane = lax.broadcasted_iota(jnp.int32, (m, 128), 1)
    out = jnp.zeros((m, 128), F32)
    for index, piece in enumerate(pieces):
        out = jnp.where(lane == index, piece, out)
    return out


def total(values):
    return jnp.sum(values, axis=1, keepdims=True)


def late_other_kernel(n, u_ref, be_ref, bl_ref, ye_ref, yl_ref, k_ref, y_ref, a, v):
    fill([u_ref], n, 0, a)
    vectors([u_ref], n, v)
    early = be_ref.shape[0]
    k_ref[:, :early] = tile(a[...], be_ref[...])
    k_ref[:, early:] = tile(a[...], bl_ref[...])
    y_ref[:, :early] = ye_ref[...] + across_rows(v[...], k_ref[:, :early])
    y_ref[:, early:] = yl_ref[...] + across_rows(v[...], k_ref[:, early:])


def targets_kernel(n, z_ref, x_ref, late_ref, u_ref, late_u_ref, mine_ref, theirs_ref):
    vectors([z_ref, x_ref, late_ref], n, mine_ref, low=True)
    vectors([u_ref, late_u_ref], n, theirs_ref, low=True)


def both(values):
    return total(values[0]) + total(values[1])


def second_kernel(
    n, b_ref, bu_ref, y_ref, yu_ref, ke_ref, keu_ref, kl_ref, ku_ref, z_ref, sums_ref, p_ref, pu_ref
):
    early = ke_ref.shape[0]
    b = (b_ref[...], bu_ref[...])
    w = tuple(y[...] + noise_level * v for y, v in zip((y_ref, yu_ref), b))
    bb = both([v * v for v in b])
    a0 = bb / both([v * u for v, u in zip(b, w)])
    r = [v - a0 * u for v, u in zip(b, w)]
    rr = both([v * v for v in r])
    beta = rr / bb
    p = r[0] + beta * b[0]
    p_ref[...] = p.astype(BF16)
    pu_ref[...] = (r[1] + beta * b[1]).astype(BF16)
    pe, pl_, ue, ul = p_ref[:, :early], p_ref[:, early:], pu_ref[:, :early], pu_ref[:, early:]
    ze = (
        across_rows(pe, ke_ref[...])
        + across_columns(pl_, kl_ref[:early])
        + across_rows(ue, keu_ref[...])
        + across_rows(ul, ku_ref[:, :early])
    ) + noise_level * p[:, :early]
    zl = (
        across_rows(pe, kl_ref[:early])
        + across_rows(ue, kl_ref[early : 2 * early])
        + across_rows(pl_, kl_ref[2 * early :])
        + across_rows(ul, ku_ref[:, early:])
    ) + noise_level * p[:, early:]
    z_ref[...] = ze[:, :n]
    pz = total(p[:, :early] * ze) + total(p[:, early:] * zl)
    sums_ref[...] = columns_of([pz, a0, beta, rr], y_ref.shape[0])


def last_kernel(n, b_ref, y_ref, image_ref, mine_ref, theirs_ref, x_ref, r_ref):
    a0, beta, rr = (mine_ref[:, i : i + 1] for i in (1, 2, 3))
    a1 = rr / (mine_ref[:, 0:1] + theirs_ref[:, 0:1])
    b = b_ref[...]
    r = b - a0 * (y_ref[:, :n] + noise_level * b)
    p = r + beta * b
    x_ref[...] = a0 * b + a1 * p
    r_ref[...] = r - a1 * image_ref[...]


def pair_body(points, inv_scale, targets):
    n, depth = points.shape
    m = targets.shape[1]
    own = targets.T
    early, late = 6 * n, 2 * n

    def along(x, step):
        return lax.ppermute(x, "blk", [(i, i ^ step) for i in range(4)])

    def across(x):
        return lax.ppermute(x, "narrow", [(i, i ^ 2) for i in range(4)])

    def swap(x):
        return lax.ppermute(x, "narrow", [(i, i ^ 1) for i in range(4)])

    def f32(*shape):
        return jax.ShapeDtypeStruct(shape, F32)

    def bf16(*shape):
        return jax.ShapeDtypeStruct(shape, BF16)

    def named(kernel, outs, name, tiles=0, scratch=()):
        return call(
            functools.partial(kernel, n), outs, name,
            flops=tiles * (4 * depth + 2 * m), exps=tiles, bytes_=2 * tiles, scratch=scratch,
        )

    scaled = (points.astype(F32) * inv_scale[None, :]).astype(BF16)
    high = lax.reduce_precision(own, 8, 7)
    low = (own - high).astype(BF16)
    high = high.astype(BF16)
    half = n // 2
    pack = jnp.concatenate(
        [scaled, high[:, :half], high[:, half:], low[:, :half], low[:, half:]], axis=0
    )
    far = [along(pack, 3), along(pack, 2)]
    next_ = along(pack, 1)
    x_own = across(pack)
    x_next = across(next_)
    late_z = jnp.concatenate(far, axis=0)
    late_x = across(late_z)
    z_all = jnp.concatenate([pack, next_, late_z], axis=0)
    early_x = jnp.concatenate([x_own, x_next], axis=0)
    early_u = swap(jnp.concatenate([z_all, early_x], axis=0))
    a_e, b_e, v_e, k_e, y_e = named(
        early_kernel,
        (bf16(early, 2 * depth), bf16(early, 2 * depth), bf16(m, early), bf16(early, early), f32(m, early)),
        "early", early * early,
    )(z_all, early_x)
    a_u, v_u, k_eu, y_e = named(
        early_other_kernel,
        (bf16(early, 2 * depth), bf16(m, early), bf16(early, early), f32(m, early)),
        "early_other", early * early,
    )(early_u, b_e, y_e)
    late_x, y_e = lax.optimization_barrier((late_x, y_e))
    late_u = swap(late_x)
    b_l, v_l, k_l, y_e, y_l = named(
        late_kernel,
        (bf16(late, 2 * depth), bf16(m, late), bf16(2 * early + late, late), f32(m, early), f32(m, late)),
        "late", (2 * early + late) * late,
        scratch=[pltpu.VMEM((late, 2 * depth), BF16)],
    )(late_x, a_e, a_u, v_e, v_u, y_e)
    k_u, y = named(
        late_other_kernel,
        (bf16(late, early + late), f32(m, early + late)),
        "late_other", late * (early + late),
        scratch=[pltpu.VMEM((late, 2 * depth), BF16), pltpu.VMEM((m, late), BF16)],
    )(late_u, b_e, b_l, y_e, y_l)
    y_u = swap(y)
    b, b_u = named(targets_kernel, (f32(m, early + late), f32(m, early + late)), "targets")(
        z_all, early_x, late_x, early_u, late_u
    )
    image, sums = named(
        second_kernel, (f32(m, n), f32(m, 128)), "second",
        scratch=[pltpu.VMEM((m, early + late), BF16), pltpu.VMEM((m, early + late), BF16)],
    )(b, b_u, y, y_u, k_e, k_eu, k_l, k_u)
    sums_u = swap(sums)
    x, r = named(last_kernel, (f32(m, n), f32(m, n)), "last")(own, y, image, sums, sums_u)
    return x.T, r.T


def spread_body(points, inv_scale, targets):
    def column_total(values):
        return lax.psum(jnp.sum(values, axis=0), ("blk", "narrow"))

    scaled = (points.astype(F32) * inv_scale[None, :]).astype(BF16)
    rows = lax.all_gather(scaled, "narrow", axis=0, tiled=True)
    columns = lax.all_gather(scaled, "blk", axis=0, tiled=True)
    row_sq = jnp.sum(jnp.square(rows.astype(F32)), axis=1)
    col_sq = jnp.sum(jnp.square(columns.astype(F32)), axis=1)
    inner = lax.dot_general(rows, columns, LAST, preferred_element_type=F32)
    kernel = jnp.exp(-0.5 * (row_sq[:, None] + col_sq[None, :] - 2.0 * inner)).astype(BF16)
    answer = jnp.zeros_like(targets)
    residual = targets
    direction = targets
    norm_now = column_total(residual * residual)
    for step in range(ITERATIONS):
        vector = lax.all_gather(direction.astype(BF16), "blk", axis=0, tiled=True)
        image = jnp.dot(kernel, vector, preferred_element_type=F32)
        image = lax.psum_scatter(image, "narrow", scatter_dimension=0, tiled=True)
        image = image + noise_level * direction
        alpha = norm_now / column_total(direction * image)
        answer = answer + alpha[None, :] * direction
        residual = residual - alpha[None, :] * image
        if step + 1 < ITERATIONS:
            norm_next = column_total(residual * residual)
            direction = residual + (norm_next / norm_now)[None, :] * direction
            norm_now = norm_next
    return answer, residual


def solution(mesh):
    blocks, narrow = mesh.shape["blk"], mesh.shape["narrow"]
    sharded = P(("groups", "blk", "narrow"), None)

    def whole(points, inv_scale, targets):
        n = points.shape[0] // mesh.size
        fits = narrow == 4 and blocks == 4 and n <= 256 and n == 4 * targets.shape[1]
        body = pair_body if fits else spread_body
        return jax.shard_map(
            body,
            mesh=mesh,
            in_specs=(sharded, P(), sharded),
            out_specs=(sharded, sharded),
            check_vma=False,
        )(points, inv_scale, targets)

    return whole
```

```python
import functools

import jax
import jax.numpy as jnp
from jax import lax
from jax.experimental import pallas as pl
from jax.experimental.pallas import tpu as pltpu
from jax.sharding import PartitionSpec as P

ITERATIONS = 2
noise_level = 1.0

BF16 = jnp.bfloat16
F32 = jnp.float32
LAST = (((1,), (1,)), ((), ()))
VMEM = pl.BlockSpec(memory_space=pltpu.VMEM)
LIMIT = 20 * 2**20


def call(kernel, outs, name, flops=0, exps=0, bytes_=0, scratch=()):
    return pl.pallas_call(
        kernel,
        out_shape=outs,
        out_specs=jax.tree.map(lambda _: VMEM, outs),
        scratch_shapes=list(scratch),
        name=name,
        cost_estimate=pl.CostEstimate(
            flops=flops, bytes_accessed=bytes_, transcendentals=exps
        ),
        compiler_params=pltpu.CompilerParams(vmem_limit_bytes=LIMIT),
    )


def exponents(points, first):
    n, depth = points.shape
    value = -0.5 * jnp.sum(jnp.square(points.astype(F32)), axis=1, keepdims=True)
    high = value.astype(BF16).astype(F32)
    rest = value - high
    middle = rest.astype(BF16).astype(F32)
    low = rest - middle
    lane = lax.broadcasted_iota(jnp.int32, (n, depth), 1) - first
    other = lax.broadcasted_iota(jnp.int32, (n, depth), 1) - (3 - first)
    ones = jnp.where((other >= 0) & (other < 3), 1.0, 0.0)
    terms = jnp.where(lane == 0, high, jnp.where(lane == 1, middle, jnp.where(lane == 2, low, ones)))
    return terms.astype(BF16)


def fill(packs, n, first, out):
    depth = packs[0].shape[1]
    at = 0
    for ref in packs:
        for block in range(ref.shape[0] // (2 * n)):
            start = block * 2 * n
            points = ref[start : start + n]
            out[at : at + n, :depth] = points
            out[at : at + n, depth:] = exponents(points, first)
            at += n


def vectors(packs, n, out, low=False):
    at = 0
    m = n // 4
    for ref in packs:
        for block in range(ref.shape[0] // (2 * n)):
            start = block * 2 * n + n
            for part in range(2):
                value = ref[start + part * m : start + (part + 1) * m]
                if low:
                    rest = ref[start + (part + 2) * m : start + (part + 3) * m]
                    value = value.astype(F32) + rest.astype(F32)
                out[:, at : at + n // 2] = value
                at += n // 2


def tile(a, b):
    return jnp.exp(lax.dot_general(a, b, LAST, preferred_element_type=F32)).astype(BF16)


def across_rows(v, k):
    return jnp.dot(v, k, preferred_element_type=F32)


def across_columns(v, k):
    return lax.dot_general(v, k, LAST, preferred_element_type=F32)


def early_kernel(n, z_ref, x_ref, a_ref, b_ref, v_ref, k_ref, y_ref):
    fill([z_ref, x_ref], n, 0, a_ref)
    fill([z_ref, x_ref], n, 3, b_ref)
    vectors([z_ref, x_ref], n, v_ref)
    k_ref[...] = tile(a_ref[...], b_ref[...])
    y_ref[...] = across_rows(v_ref[...], k_ref[...])


def early_other_kernel(n, u_ref, b_ref, y0_ref, a_ref, v_ref, k_ref, y_ref):
    fill([u_ref], n, 0, a_ref)
    vectors([u_ref], n, v_ref)
    k_ref[...] = tile(a_ref[...], b_ref[...])
    y_ref[...] = y0_ref[...] + across_rows(v_ref[...], k_ref[...])


def late_kernel(
    n, x_ref, ae_ref, au_ref, ve_ref, vu_ref, y0_ref, b_ref, v_ref, k_ref, ye_ref, yl_ref, a
):
    fill([x_ref], n, 0, a)
    fill([x_ref], n, 3, b_ref)
    vectors([x_ref], n, v_ref)
    early = ae_ref.shape[0]
    b = b_ref[...]
    k_ref[:early] = tile(ae_ref[...], b)
    k_ref[early : 2 * early] = tile(au_ref[...], b)
    k_ref[2 * early :] = tile(a[...], b)
    ye_ref[...] = y0_ref[...] + across_columns(v_ref[...], k_ref[:early])
    yl_ref[...] = (
        across_rows(ve_ref[...], k_ref[:early])
        + across_rows(vu_ref[...], k_ref[early : 2 * early])
        + across_rows(v_ref[...], k_ref[2 * early :])
    )


def columns_of(pieces, m):
    lane = lax.broadcasted_iota(jnp.int32, (m, 128), 1)
    out = jnp.zeros((m, 128), F32)
    for index, piece in enumerate(pieces):
        out = jnp.where(lane == index, piece, out)
    return out


def total(values):
    return jnp.sum(values, axis=1, keepdims=True)


def late_other_kernel(n, u_ref, be_ref, bl_ref, ye_ref, yl_ref, k_ref, y_ref, a, v):
    fill([u_ref], n, 0, a)
    vectors([u_ref], n, v)
    early = be_ref.shape[0]
    k_ref[:, :early] = tile(a[...], be_ref[...])
    k_ref[:, early:] = tile(a[...], bl_ref[...])
    y_ref[:, :early] = ye_ref[...] + across_rows(v[...], k_ref[:, :early])
    y_ref[:, early:] = yl_ref[...] + across_rows(v[...], k_ref[:, early:])


def targets_kernel(n, z_ref, x_ref, late_ref, u_ref, late_u_ref, mine_ref, theirs_ref):
    vectors([z_ref, x_ref, late_ref], n, mine_ref, low=True)
    vectors([u_ref, late_u_ref], n, theirs_ref, low=True)


def both(values):
    return total(values[0]) + total(values[1])


def second_kernel(
    n, b_ref, bu_ref, y_ref, yu_ref, ke_ref, keu_ref, kl_ref, ku_ref, z_ref, sums_ref, p_ref, pu_ref
):
    early = ke_ref.shape[0]
    b = (b_ref[...], bu_ref[...])
    w = tuple(y[...] + noise_level * v for y, v in zip((y_ref, yu_ref), b))
    bb = both([v * v for v in b])
    a0 = bb / both([v * u for v, u in zip(b, w)])
    r = [v - a0 * u for v, u in zip(b, w)]
    rr = both([v * v for v in r])
    beta = rr / bb
    p = r[0] + beta * b[0]
    p_ref[...] = p.astype(BF16)
    pu_ref[...] = (r[1] + beta * b[1]).astype(BF16)
    pe, pl_, ue, ul = p_ref[:, :early], p_ref[:, early:], pu_ref[:, :early], pu_ref[:, early:]
    ze = (
        across_rows(pe, ke_ref[...])
        + across_columns(pl_, kl_ref[:early])
        + across_rows(ue, keu_ref[...])
        + across_rows(ul, ku_ref[:, :early])
    ) + noise_level * p[:, :early]
    zl = (
        across_rows(pe, kl_ref[:early])
        + across_rows(ue, kl_ref[early : 2 * early])
        + across_rows(pl_, kl_ref[2 * early :])
        + across_rows(ul, ku_ref[:, early:])
    ) + noise_level * p[:, early:]
    z_ref[...] = ze[:, :n]
    pz = total(p[:, :early] * ze) + total(p[:, early:] * zl)
    sums_ref[...] = columns_of([pz, a0, beta, rr], y_ref.shape[0])


def last_kernel(n, b_ref, y_ref, image_ref, mine_ref, theirs_ref, x_ref, r_ref):
    a0, beta, rr = (mine_ref[:, i : i + 1] for i in (1, 2, 3))
    a1 = rr / (mine_ref[:, 0:1] + theirs_ref[:, 0:1])
    b = b_ref[...]
    r = b - a0 * (y_ref[:, :n] + noise_level * b)
    p = r + beta * b
    x_ref[...] = a0 * b + a1 * p
    r_ref[...] = r - a1 * image_ref[...]


def pair_body(points, inv_scale, targets):
    n, depth = points.shape
    m = targets.shape[1]
    own = targets.T
    early, late = 6 * n, 2 * n

    def along(x, step):
        return lax.ppermute(x, "blk", [(i, i ^ step) for i in range(4)])

    def across(x):
        return lax.ppermute(x, "narrow", [(i, i ^ 2) for i in range(4)])

    def swap(x):
        return lax.ppermute(x, "narrow", [(i, i ^ 1) for i in range(4)])

    def f32(*shape):
        return jax.ShapeDtypeStruct(shape, F32)

    def bf16(*shape):
        return jax.ShapeDtypeStruct(shape, BF16)

    def named(kernel, outs, name, tiles=0, scratch=()):
        return call(
            functools.partial(kernel, n), outs, name,
            flops=tiles * (4 * depth + 2 * m), exps=tiles, bytes_=2 * tiles, scratch=scratch,
        )

    scaled = (points.astype(F32) * inv_scale[None, :]).astype(BF16)
    high = lax.reduce_precision(own, 8, 7)
    low = (own - high).astype(BF16)
    high = high.astype(BF16)
    half = n // 2
    pack = jnp.concatenate(
        [scaled, high[:, :half], high[:, half:], low[:, :half], low[:, half:]], axis=0
    )
    far = [along(pack, 3), along(pack, 2)]
    next_ = along(pack, 1)
    first, next_ = lax.optimization_barrier((pack, next_))
    x_own = across(first)
    x_next = across(next_)
    late_z = jnp.concatenate(far, axis=0)
    late_x = across(late_z)
    z_all = jnp.concatenate([pack, next_, late_z], axis=0)
    early_x = jnp.concatenate([x_own, x_next], axis=0)
    early_u = swap(jnp.concatenate([z_all, early_x], axis=0))
    a_e, b_e, v_e, k_e, y_e = named(
        early_kernel,
        (bf16(early, 2 * depth), bf16(early, 2 * depth), bf16(m, early), bf16(early, early), f32(m, early)),
        "early", early * early,
    )(z_all, early_x)
    a_u, v_u, k_eu, y_e = named(
        early_other_kernel,
        (bf16(early, 2 * depth), bf16(m, early), bf16(early, early), f32(m, early)),
        "early_other", early * early,
    )(early_u, b_e, y_e)
    late_x, y_e = lax.optimization_barrier((late_x, y_e))
    late_u = swap(late_x)
    b_l, v_l, k_l, y_e, y_l = named(
        late_kernel,
        (bf16(late, 2 * depth), bf16(m, late), bf16(2 * early + late, late), f32(m, early), f32(m, late)),
        "late", (2 * early + late) * late,
        scratch=[pltpu.VMEM((late, 2 * depth), BF16)],
    )(late_x, a_e, a_u, v_e, v_u, y_e)
    k_u, y = named(
        late_other_kernel,
        (bf16(late, early + late), f32(m, early + late)),
        "late_other", late * (early + late),
        scratch=[pltpu.VMEM((late, 2 * depth), BF16), pltpu.VMEM((m, late), BF16)],
    )(late_u, b_e, b_l, y_e, y_l)
    y_u = swap(y)
    b, b_u = named(targets_kernel, (f32(m, early + late), f32(m, early + late)), "targets")(
        z_all, early_x, late_x, early_u, late_u
    )
    image, sums = named(
        second_kernel, (f32(m, n), f32(m, 128)), "second",
        scratch=[pltpu.VMEM((m, early + late), BF16), pltpu.VMEM((m, early + late), BF16)],
    )(b, b_u, y, y_u, k_e, k_eu, k_l, k_u)
    sums_u = swap(sums)
    x, r = named(last_kernel, (f32(m, n), f32(m, n)), "last")(own, y, image, sums, sums_u)
    return x.T, r.T


def spread_body(points, inv_scale, targets):
    def column_total(values):
        return lax.psum(jnp.sum(values, axis=0), ("blk", "narrow"))

    scaled = (points.astype(F32) * inv_scale[None, :]).astype(BF16)
    rows = lax.all_gather(scaled, "narrow", axis=0, tiled=True)
    columns = lax.all_gather(scaled, "blk", axis=0, tiled=True)
    row_sq = jnp.sum(jnp.square(rows.astype(F32)), axis=1)
    col_sq = jnp.sum(jnp.square(columns.astype(F32)), axis=1)
    inner = lax.dot_general(rows, columns, LAST, preferred_element_type=F32)
    kernel = jnp.exp(-0.5 * (row_sq[:, None] + col_sq[None, :] - 2.0 * inner)).astype(BF16)
    answer = jnp.zeros_like(targets)
    residual = targets
    direction = targets
    norm_now = column_total(residual * residual)
    for step in range(ITERATIONS):
        vector = lax.all_gather(direction.astype(BF16), "blk", axis=0, tiled=True)
        image = jnp.dot(kernel, vector, preferred_element_type=F32)
        image = lax.psum_scatter(image, "narrow", scatter_dimension=0, tiled=True)
        image = image + noise_level * direction
        alpha = norm_now / column_total(direction * image)
        answer = answer + alpha[None, :] * direction
        residual = residual - alpha[None, :] * image
        if step + 1 < ITERATIONS:
            norm_next = column_total(residual * residual)
            direction = residual + (norm_next / norm_now)[None, :] * direction
            norm_now = norm_next
    return answer, residual


def solution(mesh):
    blocks, narrow = mesh.shape["blk"], mesh.shape["narrow"]
    sharded = P(("groups", "blk", "narrow"), None)

    def whole(points, inv_scale, targets):
        n = points.shape[0] // mesh.size
        fits = narrow == 4 and blocks == 4 and n <= 256 and n == 4 * targets.shape[1]
        body = pair_body if fits else spread_body
        return jax.shard_map(
            body,
            mesh=mesh,
            in_specs=(sharded, P(), sharded),
            out_specs=(sharded, sharded),
            check_vma=False,
        )(points, inv_scale, targets)

    return whole
```

```python
import functools

import jax
import jax.numpy as jnp
from jax import lax
from jax.experimental import pallas as pl
from jax.experimental.pallas import tpu as pltpu
from jax.sharding import PartitionSpec as P

ITERATIONS = 2
noise_level = 1.0

BF16 = jnp.bfloat16
F32 = jnp.float32
LAST = (((1,), (1,)), ((), ()))
VMEM = pl.BlockSpec(memory_space=pltpu.VMEM)
LIMIT = 20 * 2**20


def call(kernel, outs, name, flops=0, exps=0, bytes_=0, scratch=()):
    return pl.pallas_call(
        kernel,
        out_shape=outs,
        out_specs=jax.tree.map(lambda _: VMEM, outs),
        scratch_shapes=list(scratch),
        name=name,
        cost_estimate=pl.CostEstimate(
            flops=flops, bytes_accessed=bytes_, transcendentals=exps
        ),
        compiler_params=pltpu.CompilerParams(vmem_limit_bytes=LIMIT),
    )


def exponents(points, first):
    n, depth = points.shape
    value = -0.5 * jnp.sum(jnp.square(points.astype(F32)), axis=1, keepdims=True)
    high = value.astype(BF16).astype(F32)
    rest = value - high
    middle = rest.astype(BF16).astype(F32)
    low = rest - middle
    lane = lax.broadcasted_iota(jnp.int32, (n, depth), 1) - first
    other = lax.broadcasted_iota(jnp.int32, (n, depth), 1) - (3 - first)
    ones = jnp.where((other >= 0) & (other < 3), 1.0, 0.0)
    terms = jnp.where(lane == 0, high, jnp.where(lane == 1, middle, jnp.where(lane == 2, low, ones)))
    return terms.astype(BF16)


def fill(packs, n, first, out):
    depth = packs[0].shape[1]
    at = 0
    for ref in packs:
        for block in range(ref.shape[0] // (2 * n)):
            start = block * 2 * n
            points = ref[start : start + n]
            out[at : at + n, :depth] = points
            out[at : at + n, depth:] = exponents(points, first)
            at += n


def vectors(packs, n, out, low=False):
    at = 0
    m = n // 4
    for ref in packs:
        for block in range(ref.shape[0] // (2 * n)):
            start = block * 2 * n + n
            for part in range(2):
                value = ref[start + part * m : start + (part + 1) * m]
                if low:
                    rest = ref[start + (part + 2) * m : start + (part + 3) * m]
                    value = value.astype(F32) + rest.astype(F32)
                out[:, at : at + n // 2] = value
                at += n // 2


def tile(a, b):
    return jnp.exp(lax.dot_general(a, b, LAST, preferred_element_type=F32)).astype(BF16)


def across_rows(v, k):
    return jnp.dot(v, k, preferred_element_type=F32)


def across_columns(v, k):
    return lax.dot_general(v, k, LAST, preferred_element_type=F32)


def early_kernel(n, z_ref, x_ref, a_ref, b_ref, v_ref, k_ref, y_ref):
    fill([z_ref, x_ref], n, 0, a_ref)
    fill([z_ref, x_ref], n, 3, b_ref)
    vectors([z_ref, x_ref], n, v_ref)
    k_ref[...] = tile(a_ref[...], b_ref[...])
    y_ref[...] = across_rows(v_ref[...], k_ref[...])


def early_other_kernel(n, u_ref, b_ref, y0_ref, a_ref, v_ref, k_ref, y_ref):
    fill([u_ref], n, 0, a_ref)
    vectors([u_ref], n, v_ref)
    k_ref[...] = tile(a_ref[...], b_ref[...])
    y_ref[...] = y0_ref[...] + across_rows(v_ref[...], k_ref[...])


def late_kernel(
    n, x_ref, ae_ref, au_ref, ve_ref, vu_ref, y0_ref, b_ref, k_ref, ye_ref, yl_ref, a, v_ref
):
    fill([x_ref], n, 0, a)
    fill([x_ref], n, 3, b_ref)
    vectors([x_ref], n, v_ref)
    early = ae_ref.shape[0]
    b = b_ref[...]
    k_ref[:early] = tile(ae_ref[...], b)
    k_ref[early : 2 * early] = tile(au_ref[...], b)
    k_ref[2 * early :] = tile(a[...], b)
    ye_ref[...] = y0_ref[...] + across_columns(v_ref[...], k_ref[:early])
    yl_ref[...] = (
        across_rows(ve_ref[...], k_ref[:early])
        + across_rows(vu_ref[...], k_ref[early : 2 * early])
        + across_rows(v_ref[...], k_ref[2 * early :])
    )


def columns_of(pieces, m):
    lane = lax.broadcasted_iota(jnp.int32, (m, 128), 1)
    out = jnp.zeros((m, 128), F32)
    for index, piece in enumerate(pieces):
        out = jnp.where(lane == index, piece, out)
    return out


def total(values):
    return jnp.sum(values, axis=1, keepdims=True)


def late_other_kernel(n, u_ref, be_ref, bl_ref, ye_ref, yl_ref, k_ref, y_ref, a, v):
    fill([u_ref], n, 0, a)
    vectors([u_ref], n, v)
    early = be_ref.shape[0]
    k_ref[:, :early] = tile(a[...], be_ref[...])
    k_ref[:, early:] = tile(a[...], bl_ref[...])
    y_ref[:, :early] = ye_ref[...] + across_rows(v[...], k_ref[:, :early])
    y_ref[:, early:] = yl_ref[...] + across_rows(v[...], k_ref[:, early:])


def targets_kernel(n, z_ref, x_ref, late_ref, u_ref, late_u_ref, mine_ref, theirs_ref):
    vectors([z_ref, x_ref, late_ref], n, mine_ref, low=True)
    vectors([u_ref, late_u_ref], n, theirs_ref, low=True)


def both(values):
    return total(values[0]) + total(values[1])


def second_kernel(
    n, b_ref, bu_ref, y_ref, yu_ref, ke_ref, keu_ref, kl_ref, ku_ref, z_ref, sums_ref, p_ref, pu_ref
):
    early = ke_ref.shape[0]
    b = (b_ref[...], bu_ref[...])
    w = tuple(y[...] + noise_level * v for y, v in zip((y_ref, yu_ref), b))
    bb = both([v * v for v in b])
    a0 = bb / both([v * u for v, u in zip(b, w)])
    r = [v - a0 * u for v, u in zip(b, w)]
    rr = both([v * v for v in r])
    beta = rr / bb
    p = r[0] + beta * b[0]
    p_ref[...] = p.astype(BF16)
    pu_ref[...] = (r[1] + beta * b[1]).astype(BF16)
    pe, pl_, ue, ul = p_ref[:, :early], p_ref[:, early:], pu_ref[:, :early], pu_ref[:, early:]
    ze = (
        across_rows(pe, ke_ref[...])
        + across_columns(pl_, kl_ref[:early])
        + across_rows(ue, keu_ref[...])
        + across_rows(ul, ku_ref[:, :early])
    ) + noise_level * p[:, :early]
    zl = (
        across_rows(pe, kl_ref[:early])
        + across_rows(ue, kl_ref[early : 2 * early])
        + across_rows(pl_, kl_ref[2 * early :])
        + across_rows(ul, ku_ref[:, early:])
    ) + noise_level * p[:, early:]
    z_ref[...] = ze[:, :n]
    pz = total(p[:, :early] * ze) + total(p[:, early:] * zl)
    sums_ref[...] = columns_of([pz, a0, beta, rr], y_ref.shape[0])


def last_kernel(n, b_ref, y_ref, image_ref, mine_ref, theirs_ref, x_ref, r_ref):
    a0, beta, rr = (mine_ref[:, i : i + 1] for i in (1, 2, 3))
    a1 = rr / (mine_ref[:, 0:1] + theirs_ref[:, 0:1])
    b = b_ref[...]
    r = b - a0 * (y_ref[:, :n] + noise_level * b)
    p = r + beta * b
    x_ref[...] = a0 * b + a1 * p
    r_ref[...] = r - a1 * image_ref[...]


def pair_body(points, inv_scale, targets):
    n, depth = points.shape
    m = targets.shape[1]
    own = targets.T
    early, late = 6 * n, 2 * n

    def along(x, step):
        return lax.ppermute(x, "blk", [(i, i ^ step) for i in range(4)])

    def across(x):
        return lax.ppermute(x, "narrow", [(i, i ^ 2) for i in range(4)])

    def swap(x):
        return lax.ppermute(x, "narrow", [(i, i ^ 1) for i in range(4)])

    def f32(*shape):
        return jax.ShapeDtypeStruct(shape, F32)

    def bf16(*shape):
        return jax.ShapeDtypeStruct(shape, BF16)

    def named(kernel, outs, name, tiles=0, scratch=()):
        return call(
            functools.partial(kernel, n), outs, name,
            flops=tiles * (4 * depth + 2 * m), exps=tiles, bytes_=2 * tiles, scratch=scratch,
        )

    scaled = (points.astype(F32) * inv_scale[None, :]).astype(BF16)
    high = lax.reduce_precision(own, 8, 7)
    low = (own - high).astype(BF16)
    high = high.astype(BF16)
    half = n // 2
    pack = jnp.concatenate(
        [scaled, high[:, :half], high[:, half:], low[:, :half], low[:, half:]], axis=0
    )
    far = [along(pack, 3), along(pack, 2)]
    next_ = along(pack, 1)
    first, next_ = lax.optimization_barrier((pack, next_))
    x_own = across(first)
    x_next = across(next_)
    late_z = jnp.concatenate(far, axis=0)
    late_x = across(late_z)
    z_all = jnp.concatenate([pack, next_, late_z], axis=0)
    early_x = jnp.concatenate([x_own, x_next], axis=0)
    early_u = swap(jnp.concatenate([z_all, early_x], axis=0))
    a_e, b_e, v_e, k_e, y_e = named(
        early_kernel,
        (bf16(early, 2 * depth), bf16(early, 2 * depth), bf16(m, early), bf16(early, early), f32(m, early)),
        "early", early * early,
    )(z_all, early_x)
    a_u, v_u, k_eu, y_e = named(
        early_other_kernel,
        (bf16(early, 2 * depth), bf16(m, early), bf16(early, early), f32(m, early)),
        "early_other", early * early,
    )(early_u, b_e, y_e)
    late_x, y_e = lax.optimization_barrier((late_x, y_e))
    late_u = swap(late_x)
    b_l, k_l, y_e, y_l = named(
        late_kernel,
        (bf16(late, 2 * depth), bf16(2 * early + late, late), f32(m, early), f32(m, late)),
        "late", (2 * early + late) * late,
        scratch=[pltpu.VMEM((late, 2 * depth), BF16), pltpu.VMEM((m, late), BF16)],
    )(late_x, a_e, a_u, v_e, v_u, y_e)
    k_u, y = named(
        late_other_kernel,
        (bf16(late, early + late), f32(m, early + late)),
        "late_other", late * (early + late),
        scratch=[pltpu.VMEM((late, 2 * depth), BF16), pltpu.VMEM((m, late), BF16)],
    )(late_u, b_e, b_l, y_e, y_l)
    y_u = swap(y)
    b, b_u = named(targets_kernel, (f32(m, early + late), f32(m, early + late)), "targets")(
        z_all, early_x, late_x, early_u, late_u
    )
    image, sums = named(
        second_kernel, (f32(m, n), f32(m, 128)), "second",
        scratch=[pltpu.VMEM((m, early + late), BF16), pltpu.VMEM((m, early + late), BF16)],
    )(b, b_u, y, y_u, k_e, k_eu, k_l, k_u)
    sums_u = swap(sums)
    x, r = named(last_kernel, (f32(m, n), f32(m, n)), "last")(own, y, image, sums, sums_u)
    return x.T, r.T


def spread_body(points, inv_scale, targets):
    def column_total(values):
        return lax.psum(jnp.sum(values, axis=0), ("blk", "narrow"))

    scaled = (points.astype(F32) * inv_scale[None, :]).astype(BF16)
    rows = lax.all_gather(scaled, "narrow", axis=0, tiled=True)
    columns = lax.all_gather(scaled, "blk", axis=0, tiled=True)
    row_sq = jnp.sum(jnp.square(rows.astype(F32)), axis=1)
    col_sq = jnp.sum(jnp.square(columns.astype(F32)), axis=1)
    inner = lax.dot_general(rows, columns, LAST, preferred_element_type=F32)
    kernel = jnp.exp(-0.5 * (row_sq[:, None] + col_sq[None, :] - 2.0 * inner)).astype(BF16)
    answer = jnp.zeros_like(targets)
    residual = targets
    direction = targets
    norm_now = column_total(residual * residual)
    for step in range(ITERATIONS):
        vector = lax.all_gather(direction.astype(BF16), "blk", axis=0, tiled=True)
        image = jnp.dot(kernel, vector, preferred_element_type=F32)
        image = lax.psum_scatter(image, "narrow", scatter_dimension=0, tiled=True)
        image = image + noise_level * direction
        alpha = norm_now / column_total(direction * image)
        answer = answer + alpha[None, :] * direction
        residual = residual - alpha[None, :] * image
        if step + 1 < ITERATIONS:
            norm_next = column_total(residual * residual)
            direction = residual + (norm_next / norm_now)[None, :] * direction
            norm_now = norm_next
    return answer, residual


def solution(mesh):
    blocks, narrow = mesh.shape["blk"], mesh.shape["narrow"]
    sharded = P(("groups", "blk", "narrow"), None)

    def whole(points, inv_scale, targets):
        n = points.shape[0] // mesh.size
        fits = narrow == 4 and blocks == 4 and n <= 256 and n == 4 * targets.shape[1]
        body = pair_body if fits else spread_body
        return jax.shard_map(
            body,
            mesh=mesh,
            in_specs=(sharded, P(), sharded),
            out_specs=(sharded, sharded),
            check_vma=False,
        )(points, inv_scale, targets)

    return whole
```

```python
import functools

import jax
import jax.numpy as jnp
from jax import lax
from jax.experimental import pallas as pl
from jax.experimental.pallas import tpu as pltpu
from jax.sharding import PartitionSpec as P

ITERATIONS = 2
noise_level = 1.0

BF16 = jnp.bfloat16
F32 = jnp.float32
LAST = (((1,), (1,)), ((), ()))
VMEM = pl.BlockSpec(memory_space=pltpu.VMEM)
LIMIT = 20 * 2**20


def call(kernel, outs, name, flops=0, exps=0, bytes_=0, scratch=()):
    return pl.pallas_call(
        kernel,
        out_shape=outs,
        out_specs=jax.tree.map(lambda _: VMEM, outs),
        scratch_shapes=list(scratch),
        name=name,
        cost_estimate=pl.CostEstimate(
            flops=flops, bytes_accessed=bytes_, transcendentals=exps
        ),
        compiler_params=pltpu.CompilerParams(vmem_limit_bytes=LIMIT),
    )


def exponents(points, first):
    n, depth = points.shape
    value = -0.5 * jnp.sum(jnp.square(points.astype(F32)), axis=1, keepdims=True)
    high = value.astype(BF16).astype(F32)
    rest = value - high
    middle = rest.astype(BF16).astype(F32)
    low = rest - middle
    lane = lax.broadcasted_iota(jnp.int32, (n, depth), 1) - first
    other = lax.broadcasted_iota(jnp.int32, (n, depth), 1) - (3 - first)
    ones = jnp.where((other >= 0) & (other < 3), 1.0, 0.0)
    terms = jnp.where(lane == 0, high, jnp.where(lane == 1, middle, jnp.where(lane == 2, low, ones)))
    return terms.astype(BF16)


def fill(packs, n, first, out):
    depth = packs[0].shape[1]
    at = 0
    for ref in packs:
        for block in range(ref.shape[0] // (2 * n)):
            start = block * 2 * n
            points = ref[start : start + n]
            out[at : at + n, :depth] = points
            out[at : at + n, depth:] = exponents(points, first)
            at += n


def vectors(packs, n, out, low=False):
    at = 0
    m = n // 4
    for ref in packs:
        for block in range(ref.shape[0] // (2 * n)):
            start = block * 2 * n + n
            for part in range(2):
                value = ref[start + part * m : start + (part + 1) * m]
                if low:
                    rest = ref[start + (part + 2) * m : start + (part + 3) * m]
                    value = value.astype(F32) + rest.astype(F32)
                out[:, at : at + n // 2] = value
                at += n // 2


def tile(a, b):
    return jnp.exp(lax.dot_general(a, b, LAST, preferred_element_type=F32)).astype(BF16)


def across_rows(v, k):
    return jnp.dot(v, k, preferred_element_type=F32)


def across_columns(v, k):
    return lax.dot_general(v, k, LAST, preferred_element_type=F32)


def early_kernel(n, z_ref, x_ref, a_ref, b_ref, v_ref, k_ref, y_ref):
    fill([z_ref, x_ref], n, 0, a_ref)
    fill([z_ref, x_ref], n, 3, b_ref)
    vectors([z_ref, x_ref], n, v_ref)
    k_ref[...] = tile(a_ref[...], b_ref[...])
    y_ref[...] = across_rows(v_ref[...], k_ref[...])


def early_other_kernel(n, u_ref, b_ref, y0_ref, a_ref, v_ref, k_ref, y_ref):
    fill([u_ref], n, 0, a_ref)
    vectors([u_ref], n, v_ref)
    k_ref[...] = tile(a_ref[...], b_ref[...])
    y_ref[...] = y0_ref[...] + across_rows(v_ref[...], k_ref[...])


def late_kernel(
    n, x_ref, ae_ref, au_ref, ve_ref, vu_ref, y0_ref, a, b_ref, k_ref, ye_ref, yl_ref, v_ref
):
    fill([x_ref], n, 0, a)
    fill([x_ref], n, 3, b_ref)
    vectors([x_ref], n, v_ref)
    early = ae_ref.shape[0]
    b = b_ref[...]
    k_ref[:early] = tile(ae_ref[...], b)
    k_ref[early : 2 * early] = tile(au_ref[...], b)
    k_ref[2 * early :] = tile(a[...], b)
    ye_ref[...] = y0_ref[...] + across_columns(v_ref[...], k_ref[:early])
    yl_ref[...] = (
        across_rows(ve_ref[...], k_ref[:early])
        + across_rows(vu_ref[...], k_ref[early : 2 * early])
        + across_rows(v_ref[...], k_ref[2 * early :])
    )


def columns_of(pieces, m):
    lane = lax.broadcasted_iota(jnp.int32, (m, 128), 1)
    out = jnp.zeros((m, 128), F32)
    for index, piece in enumerate(pieces):
        out = jnp.where(lane == index, piece, out)
    return out


def total(values):
    return jnp.sum(values, axis=1, keepdims=True)


def late_other_kernel(n, u_ref, be_ref, bl_ref, ye_ref, yl_ref, k_ref, y_ref, a, v):
    fill([u_ref], n, 0, a)
    vectors([u_ref], n, v)
    early = be_ref.shape[0]
    k_ref[:, :early] = tile(a[...], be_ref[...])
    k_ref[:, early:] = tile(a[...], bl_ref[...])
    y_ref[:, :early] = ye_ref[...] + across_rows(v[...], k_ref[:, :early])
    y_ref[:, early:] = yl_ref[...] + across_rows(v[...], k_ref[:, early:])


def targets_kernel(
    n, z_ref, x_ref, late_ref, u_ref, late_u_ref, a_ref, b_ref, mine_ref, theirs_ref, k_ref
):
    k_ref[...] = tile(a_ref[...], b_ref[...])
    vectors([z_ref, x_ref, late_ref], n, mine_ref, low=True)
    vectors([u_ref, late_u_ref], n, theirs_ref, low=True)


def both(values):
    return total(values[0]) + total(values[1])


def second_kernel(
    n, b_ref, bu_ref, y_ref, yu_ref, ke_ref, keu_ref, kl_ref, ku_ref, kle_ref, z_ref, sums_ref, p_ref, pu_ref
):
    early = ke_ref.shape[0]
    b = (b_ref[...], bu_ref[...])
    w = tuple(y[...] + noise_level * v for y, v in zip((y_ref, yu_ref), b))
    bb = both([v * v for v in b])
    a0 = bb / both([v * u for v, u in zip(b, w)])
    r = [v - a0 * u for v, u in zip(b, w)]
    rr = both([v * v for v in r])
    beta = rr / bb
    p = r[0] + beta * b[0]
    p_ref[...] = p.astype(BF16)
    pu_ref[...] = (r[1] + beta * b[1]).astype(BF16)
    pe, pl_, ue, ul = p_ref[:, :early], p_ref[:, early:], pu_ref[:, :early], pu_ref[:, early:]
    ze = (
        across_rows(pe, ke_ref[...])
        + across_rows(pl_, kle_ref[...])
        + across_rows(ue, keu_ref[...])
        + across_rows(ul, ku_ref[:, :early])
    ) + noise_level * p[:, :early]
    zl = (
        across_rows(pe, kl_ref[:early])
        + across_rows(ue, kl_ref[early : 2 * early])
        + across_rows(pl_, kl_ref[2 * early :])
        + across_rows(ul, ku_ref[:, early:])
    ) + noise_level * p[:, early:]
    z_ref[...] = ze[:, :n]
    pz = total(p[:, :early] * ze) + total(p[:, early:] * zl)
    sums_ref[...] = columns_of([pz, a0, beta, rr], y_ref.shape[0])


def last_kernel(n, b_ref, y_ref, image_ref, mine_ref, theirs_ref, x_ref, r_ref):
    a0, beta, rr = (mine_ref[:, i : i + 1] for i in (1, 2, 3))
    a1 = rr / (mine_ref[:, 0:1] + theirs_ref[:, 0:1])
    b = b_ref[...]
    r = b - a0 * (y_ref[:, :n] + noise_level * b)
    p = r + beta * b
    x_ref[...] = a0 * b + a1 * p
    r_ref[...] = r - a1 * image_ref[...]


def pair_body(points, inv_scale, targets):
    n, depth = points.shape
    m = targets.shape[1]
    own = targets.T
    early, late = 6 * n, 2 * n

    def along(x, step):
        return lax.ppermute(x, "blk", [(i, i ^ step) for i in range(4)])

    def across(x):
        return lax.ppermute(x, "narrow", [(i, i ^ 2) for i in range(4)])

    def swap(x):
        return lax.ppermute(x, "narrow", [(i, i ^ 1) for i in range(4)])

    def f32(*shape):
        return jax.ShapeDtypeStruct(shape, F32)

    def bf16(*shape):
        return jax.ShapeDtypeStruct(shape, BF16)

    def named(kernel, outs, name, tiles=0, scratch=()):
        return call(
            functools.partial(kernel, n), outs, name,
            flops=tiles * (4 * depth + 2 * m), exps=tiles, bytes_=2 * tiles, scratch=scratch,
        )

    scaled = (points.astype(F32) * inv_scale[None, :]).astype(BF16)
    high = lax.reduce_precision(own, 8, 7)
    low = (own - high).astype(BF16)
    high = high.astype(BF16)
    half = n // 2
    pack = jnp.concatenate(
        [scaled, high[:, :half], high[:, half:], low[:, :half], low[:, half:]], axis=0
    )
    far = [along(pack, 3), along(pack, 2)]
    next_ = along(pack, 1)
    first, next_ = lax.optimization_barrier((pack, next_))
    x_own = across(first)
    x_next = across(next_)
    late_z = jnp.concatenate(far, axis=0)
    late_x = across(late_z)
    z_all = jnp.concatenate([pack, next_, late_z], axis=0)
    early_x = jnp.concatenate([x_own, x_next], axis=0)
    early_u = swap(jnp.concatenate([z_all, early_x], axis=0))
    a_e, b_e, v_e, k_e, y_e = named(
        early_kernel,
        (bf16(early, 2 * depth), bf16(early, 2 * depth), bf16(m, early), bf16(early, early), f32(m, early)),
        "early", early * early,
    )(z_all, early_x)
    a_u, v_u, k_eu, y_e = named(
        early_other_kernel,
        (bf16(early, 2 * depth), bf16(m, early), bf16(early, early), f32(m, early)),
        "early_other", early * early,
    )(early_u, b_e, y_e)
    late_x, y_e = lax.optimization_barrier((late_x, y_e))
    late_u = swap(late_x)
    a_l, b_l, k_l, y_e, y_l = named(
        late_kernel,
        (
            bf16(late, 2 * depth), bf16(late, 2 * depth), bf16(2 * early + late, late),
            f32(m, early), f32(m, late),
        ),
        "late", (2 * early + late) * late,
        scratch=[pltpu.VMEM((m, late), BF16)],
    )(late_x, a_e, a_u, v_e, v_u, y_e)
    k_u, y = named(
        late_other_kernel,
        (bf16(late, early + late), f32(m, early + late)),
        "late_other", late * (early + late),
        scratch=[pltpu.VMEM((late, 2 * depth), BF16), pltpu.VMEM((m, late), BF16)],
    )(late_u, b_e, b_l, y_e, y_l)
    y_u = swap(y)
    y, a_l = lax.optimization_barrier((y, a_l))
    b, b_u, k_le = named(
        targets_kernel,
        (f32(m, early + late), f32(m, early + late), bf16(late, early)),
        "targets", late * early,
    )(
        z_all, early_x, late_x, early_u, late_u, a_l, b_e
    )
    image, sums = named(
        second_kernel, (f32(m, n), f32(m, 128)), "second",
        scratch=[pltpu.VMEM((m, early + late), BF16), pltpu.VMEM((m, early + late), BF16)],
    )(b, b_u, y, y_u, k_e, k_eu, k_l, k_u, k_le)
    sums_u = swap(sums)
    x, r = named(last_kernel, (f32(m, n), f32(m, n)), "last")(own, y, image, sums, sums_u)
    return x.T, r.T


def spread_body(points, inv_scale, targets):
    def column_total(values):
        return lax.psum(jnp.sum(values, axis=0), ("blk", "narrow"))

    scaled = (points.astype(F32) * inv_scale[None, :]).astype(BF16)
    rows = lax.all_gather(scaled, "narrow", axis=0, tiled=True)
    columns = lax.all_gather(scaled, "blk", axis=0, tiled=True)
    row_sq = jnp.sum(jnp.square(rows.astype(F32)), axis=1)
    col_sq = jnp.sum(jnp.square(columns.astype(F32)), axis=1)
    inner = lax.dot_general(rows, columns, LAST, preferred_element_type=F32)
    kernel = jnp.exp(-0.5 * (row_sq[:, None] + col_sq[None, :] - 2.0 * inner)).astype(BF16)
    answer = jnp.zeros_like(targets)
    residual = targets
    direction = targets
    norm_now = column_total(residual * residual)
    for step in range(ITERATIONS):
        vector = lax.all_gather(direction.astype(BF16), "blk", axis=0, tiled=True)
        image = jnp.dot(kernel, vector, preferred_element_type=F32)
        image = lax.psum_scatter(image, "narrow", scatter_dimension=0, tiled=True)
        image = image + noise_level * direction
        alpha = norm_now / column_total(direction * image)
        answer = answer + alpha[None, :] * direction
        residual = residual - alpha[None, :] * image
        if step + 1 < ITERATIONS:
            norm_next = column_total(residual * residual)
            direction = residual + (norm_next / norm_now)[None, :] * direction
            norm_now = norm_next
    return answer, residual


def solution(mesh):
    blocks, narrow = mesh.shape["blk"], mesh.shape["narrow"]
    sharded = P(("groups", "blk", "narrow"), None)

    def whole(points, inv_scale, targets):
        n = points.shape[0] // mesh.size
        fits = narrow == 4 and blocks == 4 and n <= 256 and n == 4 * targets.shape[1]
        body = pair_body if fits else spread_body
        return jax.shard_map(
            body,
            mesh=mesh,
            in_specs=(sharded, P(), sharded),
            out_specs=(sharded, sharded),
            check_vma=False,
        )(points, inv_scale, targets)

    return whole
```
